1024 devices in a mesh: doc: 4 (over y), seq: 64 (over z, core), tensor: 4 (over x).
Axes of the slice: x: 4, y: 4, z: 32, core: 2. Of those that a mesh axis runs over, the one named last changes fastest.
Arguments:
- queries: bfloat16 [4, 16384, 4096], P('doc', 'seq', 'tensor'), may hold values from -400 to 400
- vision: bfloat16 [4, 64, 128, 8192], P('doc', 'seq', 'tensor'), may hold values from -6 to 6
- w_key: bfloat16 [8192, 512], P(('doc', 'seq'), 'tensor'), may hold values from -0.0625 to 0.0625
- w_value: bfloat16 [8192, 512], P(('doc', 'seq'), 'tensor'), may hold values from -0.0625 to 0.0625
- attn_gate: float32 [1], replicated, may hold values from 0.2 to 1.2
- token_image: int32 [4, 16384, 1], P('doc', 'seq'), may hold values from 0 to 63; in each aligned block of 256 rows (0 to 255, 256 to 511, ..., all dimensions but the last counted through in order) at most 8 rows name the same one
- image_owner: int32 [4, 64], P('doc'), may hold values from 0 to 63, each once within a row
- image_len: int32 [4, 64], P('doc', 'seq'), may hold values from 32 to 128, as said below
Outputs:
- gated: bfloat16 [4, 16384, 4096], P('doc', 'seq', 'tensor')
The draws below stay inside these ranges and needn't reach their ends.
Inputs may be any that keep to these rules, and one draw needn't show every extreme that they name: `token_image`: in each group, the 256 tokens of one index of seq name one image at most 8 times; some image is named exactly 8 times by some index. `image_len`: each group has some image with all 128 vision tokens valid.
All inputs are finite; a program needn't handle non-finite values.
Results may differ from the reference program's by a relative error of at most 0.012.
The reference program's roundings to bfloat16 on the way (of `keys`, `values` and `weights`) count: a program that leaves them out, or rounds other values in their place, can miss the bound.
Values may be sent and summed in bfloat16 or wider, within the bound.
No kernel may reach another device: no remote copies, remote signals or barrier semaphores. Data moves between devices by JAX's collectives and lax.ppermute only.
A program may use at most 32 MiB of HBM per device.

```python
import math
import jax
import jax.numpy as jnp
import numpy as np
from jax import lax

HEADS = 32
KVH = 4
HD = 128
VD = 8192
VTOK = 128
TOK_DEV = 256
CAP = 8
TOKENS = 16384
N_DOC = 4
N_SEQ = 64


def draw_queries(key, part):
    key = jax.random.fold_in(key, 5)
    first = jax.random.fold_in(key, 0)
    shape = (N_DOC, N_SEQ * TOK_DEV, HEADS * HD)
    return jnp.clip(jax.random.normal(first, shape, jnp.float32), -6.0, 6.0).astype(jnp.bfloat16)


def draw_image_len(key, part):
    key = jax.random.fold_in(key, 11)
    first, second = jax.random.split(key)
    base = jax.random.randint(first, (N_DOC, N_SEQ), VTOK // 4, VTOK + 1)
    chosen = jax.random.randint(second, (N_DOC, 1), 0, N_SEQ)
    full = jnp.arange(N_SEQ)[None, :] == chosen
    return jnp.where(full, VTOK, base).astype(jnp.int32)


def levels(own_key, extent, cuts, smallest, largest):
    factor_of = 1.0
    for position, parts in cuts:
        steps = jax.random.uniform(jax.random.fold_in(jax.random.fold_in(own_key, 6), position), (parts,), jnp.float32, smallest / len(cuts), largest / len(cuts))
        factor_of = factor_of * jnp.repeat(jnp.exp(steps), extent[position] // parts).reshape((-1,) + (1,) * (len(extent) - 1 - position))
    return factor_of


def routed_block(rng, own, number, rows, amount, top, bound, skew):
    ranking = jax.random.permutation(rng, amount)
    crowded, ordinary = shares(amount, rows * top, bound, skew, True), shares(amount, rows * top, bound, skew, False)
    places = jnp.arange(amount)

    def named(sizes, turn):
        used = int((sizes > 0).sum())
        fixed = max(1, used // 4)
        passed = fixed + (places - fixed + turn * (used - fixed)) % max(1, amount - fixed)
        return jnp.zeros((amount,), jnp.int32).at[ranking[jnp.where(places < fixed, places, passed)]].set(jnp.asarray(sizes, jnp.int32))

    sizes = jnp.where(number % 4 == 0, named(crowded, number // 4), named(ordinary, number - number // 4 - 1))
    mixed = jax.random.permutation(jax.random.fold_in(own, 3), amount)
    giver, taker = mixed[0:amount // 2 * 2:2], mixed[1:amount // 2 * 2:2]
    room = jnp.minimum(sizes[giver] - 1, bound - sizes[taker]) // 2
    room = jnp.where((giver == ranking[0]) | (taker == ranking[0]) | (sizes[taker] == 0), 0, jnp.maximum(room, 0))
    passed = jax.random.randint(jax.random.fold_in(own, 4), (amount // 2,), 0, 1 << 20) % (room + 1)
    sizes = sizes.at[giver].add(-passed).at[taker].add(passed)
    labels = jnp.searchsorted(jnp.cumsum(sizes), jnp.arange(rows * top), side="right").astype(jnp.int32)
    listing = labels.reshape(top, rows).T
    listing = listing[jax.random.permutation(jax.random.fold_in(own, 1), rows)]
    turn = jax.random.randint(jax.random.fold_in(own, 2), (rows, 1), 0, top)
    return jnp.take_along_axis(listing, (jnp.arange(top)[None, :] + turn) % top, axis=1)


def shares(number_of, total, most, lean, full):
    portions = [(1 << 20) // math.isqrt(grade ** lean) + 1 for grade in range(1, number_of + 1)]
    largest = most if full else min(most, max(-(-total // number_of), total * portions[0] // sum(portions)))
    least = 1 if total - largest >= number_of - 1 else 0
    given, spare = [largest] + [least] * (number_of - 1), total - largest - least * (number_of - 1)
    while spare > 0:
        free = [i for i in range(1, number_of) if given[i] < largest] or [i for i in range(1, number_of) if given[i] < most]
        mass, remaining = sum([portions[i] for i in free]), spare
        for i in free:
            addition = min(most - given[i], max(1, remaining * portions[i] // mass), spare)
            given[i] = given[i] + addition
            spare = spare - addition
    return np.array(given)


def gaussian(rng, extent, width, most, cuts=(), held_as=jnp.bfloat16):
    gain = levels(rng, extent, cuts, -0.22, 0.18) if cuts else 1.0
    entries = jax.random.normal(rng, extent, jnp.float32) * width * gain
    return jnp.minimum(jnp.maximum(entries, -most), most).astype(held_as)


def setup_inputs(seed: int = 0) -> dict:
    streams_of = jax.random.split(jax.random.key(seed), 9)
    queries = draw_queries(jax.random.fold_in(streams_of[8], 71), 0)
    vision = gaussian(streams_of[1], (N_DOC, N_SEQ, VTOK, VD), 1.0, 6.0, ((0, 4), (1, 64), (2, 4)))
    w_key = gaussian(streams_of[2], (VD, KVH * HD), VD ** -0.5, 0.0625, ((0, 256), (1, 4)))
    w_value = gaussian(streams_of[3], (VD, KVH * HD), VD ** -0.5, 0.0625, ((0, 256), (1, 4)))
    attn_gate = jnp.clip(jax.random.uniform(streams_of[4], (1,), jnp.float32, 0.2, 1.2), 0.2, 1.2)
    token_image_keys = jax.random.split(jax.random.fold_in(streams_of[5], 1), N_DOC * TOKENS // TOK_DEV)
    token_image_turns = jax.random.permutation(jax.random.fold_in(streams_of[5], 3), N_DOC * TOKENS // TOK_DEV)
    token_image = jax.vmap(lambda own, number: routed_block(jax.random.fold_in(streams_of[5], 2), own, number, TOK_DEV, N_SEQ, 1, CAP, 2))(token_image_keys, token_image_turns).reshape((N_DOC, TOKENS, 1))
    image_owner = jax.vmap(lambda own: jax.random.permutation(own, N_SEQ))(jax.random.split(streams_of[6], N_DOC)).reshape((N_DOC, N_SEQ)).astype(jnp.int32)
    image_len = draw_image_len(jax.random.fold_in(streams_of[8], 71), 0)
    return dict(queries=queries, vision=vision, w_key=w_key, w_value=w_value, attn_gate=attn_gate, token_image=token_image, image_owner=image_owner, image_len=image_len)


def head_norm(x):
    return x * lax.rsqrt(lax.optimization_barrier(jnp.mean(x * x, axis=-1, keepdims=True)) + 1e-06)

def project(image, w_key, w_value):
    keys = jnp.dot(image, w_key, preferred_element_type=jnp.float32).reshape(VTOK, KVH, HD)
    keys = head_norm(keys).astype(jnp.bfloat16)
    values = jnp.dot(image, w_value, preferred_element_type=jnp.float32).astype(jnp.bfloat16)
    return (keys, values.reshape(VTOK, KVH, HD))

def reference(queries, vision, w_key, w_value, attn_gate, token_image, image_owner, image_len):
    rows_all = N_SEQ * TOK_DEV
    blk = 32 if rows_all % 32 == 0 else rows_all
    factor = jnp.tanh(attn_gate[0])
    scale = HD ** (-0.5)
    group_size = HEADS // KVH

    def group(inputs):
        images, lens, owner, tok_img, group_q = inputs
        keys, values = lax.map(lambda image: project(image, w_key, w_value), images)
        slots = owner[tok_img[:, 0]]
        q_blocks = group_q.reshape(rows_all // blk, blk, KVH, group_size, HD)
        s_blocks = slots.reshape(rows_all // blk, blk)

        def one(pair):
            q_part, s_part = pair
            k_part = keys[s_part].astype(jnp.float32)
            v_part = values[s_part].astype(jnp.float32)
            scores = jnp.einsum('bcgd,bkcd->bcgk', q_part.astype(jnp.float32), k_part) * scale
            valid = jnp.arange(VTOK)[None, :] < lens[s_part][:, None]
            scores = jnp.where(valid[:, None, None, :], scores, -jnp.inf)
            top = lax.optimization_barrier(jnp.max(scores, axis=-1, keepdims=True))
            probs = jnp.exp(scores - top)
            total = lax.optimization_barrier(jnp.sum(probs, axis=-1))
            weights = probs.astype(jnp.bfloat16).astype(jnp.float32)
            mixed = jnp.einsum('bcgk,bkcd->bcgd', weights, v_part) / total[..., None]
            return (factor * mixed).astype(jnp.bfloat16).reshape(blk, HEADS * HD)
        out = lax.map(one, (q_blocks, s_blocks))
        return out.reshape(rows_all, HEADS * HD)
    return lax.map(group, (vision, image_len, image_owner, token_image, queries))
```

```python
import functools

import jax
import jax.numpy as jnp
from jax import lax
from jax.experimental import pallas as pl
from jax.experimental.pallas import tpu as pltpu
from jax.sharding import PartitionSpec as P

HD = 128
CAP = 8
BF = jnp.bfloat16
F32 = jnp.float32


def head_norm(x):
    return x * lax.rsqrt(jnp.mean(x * x, axis=-1, keepdims=True) + 1e-06)


def attend(lens_ref, gate_ref, q_ref, kv_ref, out_ref):
    heads = q_ref.shape[1] // HD
    vtok = kv_ref.shape[1]
    pairs = kv_ref.shape[0] // 2
    factor = jnp.tanh(jnp.full((1, HD), gate_ref[0], F32))
    shape = (heads * 2 * CAP, 2 * vtok)
    row = lax.broadcasted_iota(jnp.int32, shape, 0)
    col = lax.broadcasted_iota(jnp.int32, shape, 1)
    row_image = (row // CAP) % 2
    first = col < vtok
    key = jnp.where(first, col, col - vtok)
    same = first == (row_image == 0)

    def body(i, carry):
        rows = pl.ds(pl.multiple_of(i * 2 * CAP, 2 * CAP), 2 * CAP)
        q = jnp.concatenate([q_ref[rows, h * HD : (h + 1) * HD] for h in range(heads)], axis=0)
        kv = kv_ref[pl.ds(2 * i, 2)].reshape(2 * vtok, 2 * HD)
        k, v = kv[:, :HD], kv[:, HD:]
        s = lax.dot_general(q, k, (((1,), (1,)), ((), ())), preferred_element_type=F32)
        s = s * (HD ** -0.5)
        length = jnp.where(first, lens_ref[2 * i], lens_ref[2 * i + 1])
        s = jnp.where(same & (key < length), s, -jnp.inf)
        top = jnp.max(s, axis=1, keepdims=True)
        p = jnp.exp(s - top)
        total = jnp.sum(p, axis=1, keepdims=True)
        mixed = jnp.dot(p.astype(BF), v, preferred_element_type=F32)
        ans = (factor * (mixed / total)).astype(BF)
        for h in range(heads):
            out_ref[rows, h * HD : (h + 1) * HD] = ans[h * 2 * CAP : (h + 1) * 2 * CAP]
        return carry

    lax.fori_loop(0, pairs, body, 0)


def attention(lens, gate, q, kv):
    return pl.pallas_call(
        attend,
        out_shape=jax.ShapeDtypeStruct(q.shape, BF),
        in_specs=[
            pl.BlockSpec(memory_space=pltpu.SMEM),
            pl.BlockSpec(memory_space=pltpu.SMEM),
            pl.BlockSpec(memory_space=pltpu.VMEM),
            pl.BlockSpec(memory_space=pltpu.VMEM),
        ],
        out_specs=pl.BlockSpec(memory_space=pltpu.VMEM),
        compiler_params=pltpu.CompilerParams(vmem_limit_bytes=32 * 1024 * 1024),
    )(lens, gate, q, kv)


def chip_shift(n_seq, d):
    return [(i, (i + 2 * d) % n_seq) for i in range(n_seq)]


def shards(queries, vision, w_key, w_value, attn_gate, token_image, image_owner, image_len):
    n_doc = lax.axis_size("doc")
    n_seq = lax.axis_size("seq")
    n_z = n_seq // 2
    seq = lax.axis_index("seq")
    core = seq % 2
    z = seq // 2
    rows32, width = vision.shape[2], vision.shape[3]
    slice_w = width // n_doc
    swap = [(i, i ^ 1) for i in range(n_seq)]

    with jax.named_scope("vision_doc"):
        cols = lax.all_to_all(vision[0, 0], "doc", split_axis=1, concat_axis=0, tiled=True)
    with jax.named_scope("vision_tensor"):
        x = lax.all_gather(cols, "tensor", axis=0, tiled=True)

    wrows = w_key.shape[0]
    w = jnp.concatenate([w_key, w_value], axis=1)
    extra = jnp.broadcast_to(image_len.astype(BF), (16, w.shape[1]))
    packed = jnp.concatenate([w, extra], axis=0)
    groups = [[2 * q + c for q in range(n_z)] for c in range(2)]
    with jax.named_scope("weights_z"):
        own = lax.all_gather(packed, "seq", axis=0, tiled=False, axis_index_groups=groups)
    with jax.named_scope("weights_core"):
        other = lax.ppermute(own, "seq", swap)
    even = jnp.where(core == 0, own, other)
    odd = jnp.where(core == 0, other, own)
    both = jnp.stack([even, odd], axis=1)
    w_all = both[:, :, :wrows].reshape(n_seq * wrows, w.shape[1])
    lens = both[:, :, wrows, 0].reshape(n_seq).astype(jnp.int32)

    with jax.named_scope("project"):
        part = jnp.dot(x, w_all, preferred_element_type=F32)
    with jax.named_scope("reduce_doc"):
        part = part.reshape(-1, n_doc, rows32, w.shape[1])
        part = lax.all_to_all(part, "doc", split_axis=1, concat_axis=1, tiled=True)
        kv = jnp.sum(part, axis=1).reshape(-1, w.shape[1])
    kv = jnp.concatenate([head_norm(kv[:, :HD]), kv[:, HD:]], axis=1).astype(BF)

    with jax.named_scope("kv_far"):
        far = [[2 * (a + 8 * j) + c for j in range(n_z // 8)] for a in range(8) for c in range(2)]
        s0 = lax.all_gather(kv, "seq", axis=0, tiled=False, axis_index_groups=far)
    nj = s0.shape[0]
    with jax.named_scope("kv_mid"):
        p3 = lax.ppermute(s0, "seq", chip_shift(n_seq, -3))
        m3 = lax.ppermute(s0, "seq", chip_shift(n_seq, 3))
    with jax.named_scope("kv_near"):
        h = nj // 2
        up = lax.ppermute(jnp.concatenate([s0, m3, p3[:h]], axis=0), "seq", chip_shift(n_seq, -1))
        dn = lax.ppermute(jnp.concatenate([m3[h:], s0, p3], axis=0), "seq", chip_shift(n_seq, 1))
    mine = jnp.concatenate([s0, p3, m3, up, dn], axis=0)
    classes = [0, 3, 5, 1, 6, 4, 7, 2]
    with jax.named_scope("kv_core"):
        theirs = lax.ppermute(mine, "seq", swap)
    kv_all = jnp.concatenate([mine, theirs], axis=0)

    owners = jnp.arange(n_seq, dtype=jnp.int32)
    oz, oc = owners // 2, owners % 2
    delta = (oz - z) % 8
    place_of = sum(jnp.where(delta == c, i, 0) for i, c in enumerate(classes))
    pos = place_of * nj + oz // 8 + n_z * (oc != core).astype(jnp.int32)
    at = owners[:, None] == pos[None, :]
    lens_at = jnp.sum(jnp.where(at, lens[None, :], 0), axis=1)

    image_ids = token_image[0, :, 0]
    owner_pos = jnp.sum(
        jnp.where(image_owner[0][:, None] == owners[None, :], pos[None, :], 0), axis=1
    )
    picked = image_ids[:, None] == owners[None, :]
    target = jnp.sum(jnp.where(picked, owner_pos[None, :], 0), axis=1)
    onehot = (target[:, None] == owners[None, :]).astype(jnp.int32)
    ranks = jnp.cumsum(onehot, axis=0) - onehot
    slot = target * CAP + jnp.sum(ranks * onehot, axis=1)
    dispatch = (slot[:, None] == jnp.arange(n_seq * CAP, dtype=jnp.int32)[None, :]).astype(BF)
    with jax.named_scope("dispatch"):
        q = jnp.dot(dispatch.T, queries[0], preferred_element_type=F32).astype(BF)
    with jax.named_scope("attention"):
        answer = attention(lens_at, attn_gate, q, kv_all)
    with jax.named_scope("combine"):
        out = jnp.dot(dispatch, answer, preferred_element_type=F32)
    return out.astype(BF)[None]


def solution(mesh):
    placed = (
        P("doc", "seq", "tensor"),
        P("doc", "seq", "tensor", None),
        P(("doc", "seq"), "tensor"),
        P(("doc", "seq"), "tensor"),
        P(),
        P("doc", "seq", None),
        P("doc", None),
        P("doc", "seq"),
    )
    return jax.shard_map(
        shards, mesh=mesh, in_specs=placed, out_specs=P("doc", "seq", "tensor"), check_vma=False
    )
```

```python
import functools

import jax
import jax.numpy as jnp
from jax import lax
from jax.experimental import pallas as pl
from jax.experimental.pallas import tpu as pltpu
from jax.sharding import PartitionSpec as P

HD = 128
CAP = 8
BF = jnp.bfloat16
F32 = jnp.float32


def head_norm(x):
    return x * lax.rsqrt(jnp.mean(x * x, axis=-1, keepdims=True) + 1e-06)


def project(place_ref, x_ref, own_ref, other_ref, out_ref, w_ref):
    rows = w_ref.shape[0] // (own_ref.shape[0] * 2)
    half = own_ref.shape[0] // 2
    core, odd = place_ref[0], place_ref[1]
    for k, ref in enumerate((own_ref, other_ref)):
        for o in range(2):
            for j in range(half):
                owner = 2 * (2 * j + (o + odd) % 2) + (k + core) % 2
                at = pl.ds(pl.multiple_of(owner * rows, rows), rows)
                w_ref[at] = ref[o * half + j, :rows]
    out_ref[...] = jnp.dot(x_ref[...], w_ref[...], preferred_element_type=F32)


def projection(place, x, own, other):
    cols = own.shape[2]
    return pl.pallas_call(
        project,
        out_shape=jax.ShapeDtypeStruct((x.shape[0], cols), F32),
        in_specs=[pl.BlockSpec(memory_space=pltpu.SMEM)]
        + [pl.BlockSpec(memory_space=pltpu.VMEM)] * 3,
        out_specs=pl.BlockSpec(memory_space=pltpu.VMEM),
        scratch_shapes=[pltpu.VMEM((x.shape[1], cols), BF)],
        compiler_params=pltpu.CompilerParams(vmem_limit_bytes=32 * 1024 * 1024),
    )(place, x, own, other)


UNROLL = 4


def attend(lens_ref, gate_ref, q_ref, kv_ref, out_ref):
    heads = q_ref.shape[1] // HD
    vtok = kv_ref.shape[1]
    pairs = kv_ref.shape[0] // 2
    factor = jnp.tanh(jnp.full((1, 1), gate_ref[0], F32))
    col = lax.broadcasted_iota(jnp.int32, (1, 2 * vtok), 1)

    def one(i):
        rows = pl.ds(pl.multiple_of(i * 2 * CAP, 2 * CAP), 2 * CAP)
        q = jnp.concatenate([q_ref[rows, h * HD : (h + 1) * HD] for h in range(heads)], axis=0)
        kv = kv_ref[pl.ds(2 * i, 2)].reshape(2 * vtok, 2 * HD)
        k, v = kv[:, :HD], kv[:, HD:]
        s = lax.dot_general(q, k, (((1,), (1,)), ((), ())), preferred_element_type=F32)
        s = s.reshape(heads, 2, CAP, 2 * vtok) * (HD ** -0.5)
        last = vtok + lens_ref[2 * i + 1]
        ok0 = col < lens_ref[2 * i]
        ok1 = (col >= vtok) & (col < last)
        s0 = jnp.where(ok0[None], s[:, 0], -jnp.inf)
        s1 = jnp.where(ok1[None], s[:, 1], -jnp.inf)
        s = jnp.stack([s0, s1], axis=1).reshape(heads * 2 * CAP, 2 * vtok)
        top = jnp.max(s, axis=1, keepdims=True)
        p = jnp.exp(s - top)
        total = jnp.sum(p, axis=1, keepdims=True)
        mixed = jnp.dot(p.astype(BF), v, preferred_element_type=F32)
        ans = (mixed * (factor / total)).astype(BF)
        for h in range(heads):
            out_ref[rows, h * HD : (h + 1) * HD] = ans[h * 2 * CAP : (h + 1) * 2 * CAP]

    def body(i, carry):
        for u in range(UNROLL):
            one(i * UNROLL + u)
        return carry

    lax.fori_loop(0, pairs // UNROLL, body, 0)


def attention(lens, gate, q, kv):
    return pl.pallas_call(
        attend,
        out_shape=jax.ShapeDtypeStruct(q.shape, BF),
        in_specs=[
            pl.BlockSpec(memory_space=pltpu.SMEM),
            pl.BlockSpec(memory_space=pltpu.SMEM),
            pl.BlockSpec(memory_space=pltpu.VMEM),
            pl.BlockSpec(memory_space=pltpu.VMEM),
        ],
        out_specs=pl.BlockSpec(memory_space=pltpu.VMEM),
        compiler_params=pltpu.CompilerParams(vmem_limit_bytes=32 * 1024 * 1024),
    )(lens, gate, q, kv)


def chip_shift(n_seq, d):
    return [(i, (i + 2 * d) % n_seq) for i in range(n_seq)]


def shards(queries, vision, w_key, w_value, attn_gate, token_image, image_owner, image_len):
    n_doc = lax.axis_size("doc")
    n_seq = lax.axis_size("seq")
    n_z = n_seq // 2
    seq = lax.axis_index("seq")
    core = seq % 2
    z = seq // 2
    rows32, width = vision.shape[2], vision.shape[3]
    slice_w = width // n_doc
    swap = [(i, i ^ 1) for i in range(n_seq)]

    with jax.named_scope("vision_doc"):
        cols = lax.all_to_all(vision[0, 0], "doc", split_axis=1, concat_axis=0, tiled=True)
    with jax.named_scope("vision_tensor"):
        x = lax.all_gather(cols, "tensor", axis=0, tiled=True)

    wrows = w_key.shape[0]
    w = jnp.concatenate([w_key, w_value], axis=1)
    extra = jnp.broadcast_to(image_len.astype(BF), (16, w.shape[1]))
    packed = jnp.concatenate([w, extra], axis=0)
    groups = [[2 * (2 * j + o) + c for j in range(n_z // 2)] for o in range(2) for c in range(2)]
    with jax.named_scope("weights_z"):
        near = lax.all_gather(packed, "seq", axis=0, tiled=False, axis_index_groups=groups)
    with jax.named_scope("weights_pair"):
        beside = lax.ppermute(near, "seq", [(i, i ^ 2) for i in range(n_seq)])
    own = jnp.concatenate([near, beside], axis=0)
    with jax.named_scope("weights_core"):
        other = lax.ppermute(own, "seq", swap)
    with jax.named_scope("project"):
        part = projection(jnp.stack([core, z % 2]), x, own, other)
    with jax.named_scope("reduce_doc"):
        part = part.reshape(-1, n_doc, rows32, w.shape[1])
        part = lax.all_to_all(part, "doc", split_axis=1, concat_axis=1, tiled=True)
        kv = jnp.sum(part, axis=1).reshape(-1, w.shape[1])
    kv = jnp.concatenate([head_norm(kv[:, :HD]), kv[:, HD:]], axis=1).astype(BF)

    with jax.named_scope("kv_far"):
        far = [[2 * (a + 8 * j) + c for j in range(n_z // 8)] for a in range(8) for c in range(2)]
        s0 = lax.all_gather(kv, "seq", axis=0, tiled=False, axis_index_groups=far)
    nj = s0.shape[0]
    with jax.named_scope("kv_mid"):
        p3 = lax.ppermute(s0, "seq", chip_shift(n_seq, -3))
        m3 = lax.ppermute(s0, "seq", chip_shift(n_seq, 3))
    with jax.named_scope("kv_near"):
        h = nj // 2
        up = lax.ppermute(jnp.concatenate([s0, m3, p3[:h]], axis=0), "seq", chip_shift(n_seq, -1))
        dn = lax.ppermute(jnp.concatenate([m3[h:], s0, p3], axis=0), "seq", chip_shift(n_seq, 1))
    mine = jnp.concatenate([s0, p3, m3, up, dn], axis=0)
    classes = [0, 3, 5, 1, 6, 4, 7, 2]
    with jax.named_scope("kv_core"):
        theirs = lax.ppermute(mine, "seq", swap)
    kv_all = jnp.concatenate([mine, theirs], axis=0)

    owners = jnp.arange(n_seq, dtype=jnp.int32)
    oz, oc = owners // 2, owners % 2
    delta = (oz - z) % 8
    place_of = sum(jnp.where(delta == c, i, 0) for i, c in enumerate(classes))
    pos = place_of * nj + oz // 8 + n_z * (oc != core).astype(jnp.int32)
    at = owners[:, None] == pos[None, :]
    lens = jnp.concatenate([own[:, wrows, 0], other[:, wrows, 0]]).astype(jnp.int32)
    from_w = n_z * (oc != core).astype(jnp.int32) + (n_z // 2) * ((oz - z) % 2) + oz // 2
    lens = jnp.sum(jnp.where(from_w[:, None] == owners[None, :], lens[None, :], 0), axis=1)
    lens_at = jnp.sum(jnp.where(at, lens[None, :], 0), axis=1)

    image_ids = token_image[0, :, 0]
    owner_pos = jnp.sum(
        jnp.where(image_owner[0][:, None] == owners[None, :], pos[None, :], 0), axis=1
    )
    picked = image_ids[:, None] == owners[None, :]
    target = jnp.sum(jnp.where(picked, owner_pos[None, :], 0), axis=1)
    onehot = (target[:, None] == owners[None, :]).astype(jnp.int32)
    ranks = jnp.cumsum(onehot, axis=0) - onehot
    slot = target * CAP + jnp.sum(ranks * onehot, axis=1)
    dispatch = (slot[:, None] == jnp.arange(n_seq * CAP, dtype=jnp.int32)[None, :]).astype(BF)
    with jax.named_scope("dispatch"):
        q = jnp.dot(dispatch.T, queries[0], preferred_element_type=F32).astype(BF)
    with jax.named_scope("attention"):
        answer = attention(lens_at, attn_gate, q, kv_all)
    with jax.named_scope("combine"):
        out = jnp.dot(dispatch, answer, preferred_element_type=F32)
    return out.astype(BF)[None]


def solution(mesh):
    placed = (
        P("doc", "seq", "tensor"),
        P("doc", "seq", "tensor", None),
        P(("doc", "seq"), "tensor"),
        P(("doc", "seq"), "tensor"),
        P(),
        P("doc", "seq", None),
        P("doc", None),
        P("doc", "seq"),
    )
    return jax.shard_map(
        shards, mesh=mesh, in_specs=placed, out_specs=P("doc", "seq", "tensor"), check_vma=False
    )
```

```python
import jax
import jax.numpy as jnp
import numpy as np
from jax import lax
from jax.experimental import pallas as pl
from jax.experimental.pallas import tpu as pltpu
from jax.sharding import PartitionSpec as P

HD = 128
CAP = 8
BF = jnp.bfloat16
F32 = jnp.float32


def head_norm(x):
    return x * lax.rsqrt(jnp.mean(x * x, axis=-1, keepdims=True) + 1e-06)


def project(place_ref, x_ref, own_ref, other_ref, out_ref, w_ref):
    @pl.when(pl.program_id(0) == 0)
    def _():
        rows = w_ref.shape[0] // (own_ref.shape[0] * 2)
        half = own_ref.shape[0] // 2
        core, odd = place_ref[0], place_ref[1]
        for k, ref in enumerate((own_ref, other_ref)):
            for o in range(2):
                for j in range(half):
                    owner = 2 * (2 * j + (o + odd) % 2) + (k + core) % 2
                    at = pl.ds(pl.multiple_of(owner * rows, rows), rows)
                    w_ref[at] = ref[o * half + j, :rows]

    out_ref[...] = jnp.dot(x_ref[...], w_ref[...], preferred_element_type=F32)


def projection(place, x, own, other, steps=4):
    rows, cols = x.shape[0] // steps, own.shape[2]
    whole = pl.BlockSpec(own.shape, lambda i: (0, 0, 0))
    return pl.pallas_call(
        project,
        grid=(steps,),
        out_shape=jax.ShapeDtypeStruct((x.shape[0], cols), F32),
        in_specs=[
            pl.BlockSpec(memory_space=pltpu.SMEM),
            pl.BlockSpec((rows, x.shape[1]), lambda i: (i, 0)),
            whole,
            whole,
        ],
        out_specs=pl.BlockSpec((rows, cols), lambda i: (i, 0)),
        scratch_shapes=[pltpu.VMEM((x.shape[1], cols), BF)],
        compiler_params=pltpu.CompilerParams(vmem_limit_bytes=48 * 1024 * 1024),
    )(place, x, own, other)


def attend(lens_ref, gate_ref, q_ref, own_ref, other_ref, out_ref):
    heads = q_ref.shape[1] // HD
    vtok = own_ref.shape[1]
    pairs = own_ref.shape[0]
    factor = jnp.tanh(jnp.full((1, 1), gate_ref[0], F32))
    col = lax.broadcasted_iota(jnp.int32, (1, 2 * vtok), 1)

    def one(i):
        rows = pl.ds(pl.multiple_of(i * 2 * CAP, 2 * CAP), 2 * CAP)
        q = jnp.concatenate([q_ref[rows, h * HD : (h + 1) * HD] for h in range(heads)], axis=0)
        kv = jnp.concatenate([own_ref[i], other_ref[i]], axis=0)
        k, v = kv[:, :HD], kv[:, HD:]
        s = lax.dot_general(q, k, (((1,), (1,)), ((), ())), preferred_element_type=F32)
        s = s.reshape(heads, 2, CAP, 2 * vtok) * (HD ** -0.5)
        ok0 = col < lens_ref[2 * i]
        ok1 = (col >= vtok) & (col < vtok + lens_ref[2 * i + 1])
        s0 = jnp.where(ok0[None], s[:, 0], -jnp.inf)
        s1 = jnp.where(ok1[None], s[:, 1], -jnp.inf)
        s = jnp.stack([s0, s1], axis=1).reshape(heads * 2 * CAP, 2 * vtok)
        top = jnp.max(s, axis=1, keepdims=True)
        p = jnp.exp(s - top)
        total = jnp.sum(p, axis=1, keepdims=True)
        mixed = jnp.dot(p.astype(BF), v, preferred_element_type=F32)
        ans = (mixed * (factor / total)).astype(BF)
        for h in range(heads):
            out_ref[rows, h * HD : (h + 1) * HD] = ans[h * 2 * CAP : (h + 1) * 2 * CAP]

    unroll = next(u for u in (4, 3, 1) if pairs % u == 0)
    if pairs < 12:
        unroll = pairs

    def body(i, carry):
        for u in range(unroll):
            one(i * unroll + u)
        return carry

    lax.fori_loop(0, pairs // unroll, body, 0)


def attention(lens, gate, q, own, other):
    smem = pl.BlockSpec(memory_space=pltpu.SMEM)
    vmem = pl.BlockSpec(memory_space=pltpu.VMEM)
    heads = q.shape[1] // HD
    pairs, vtok = own.shape[0], own.shape[1]
    scores = heads * 2 * CAP * 2 * vtok * pairs
    return pl.pallas_call(
        attend,
        out_shape=jax.ShapeDtypeStruct(q.shape, BF),
        in_specs=[smem, smem, vmem, vmem, vmem],
        out_specs=vmem,
        cost_estimate=pl.CostEstimate(
            flops=4 * scores * HD, bytes_accessed=4 * own.size * 2, transcendentals=scores
        ),
        compiler_params=pltpu.CompilerParams(vmem_limit_bytes=32 * 1024 * 1024),
    )(lens, gate, q, own, other)


def chip_shift(n_seq, d):
    return [(i, (i + 2 * d) % n_seq) for i in range(n_seq)]


def shards(queries, vision, w_key, w_value, attn_gate, token_image, image_owner, image_len):
    n_doc = lax.axis_size("doc")
    n_seq = lax.axis_size("seq")
    n_z = n_seq // 2
    seq = lax.axis_index("seq")
    core = seq % 2
    z = seq // 2
    rows32, width = vision.shape[2], vision.shape[3]
    slice_w = width // n_doc
    swap = [(i, i ^ 1) for i in range(n_seq)]

    with jax.named_scope("vision_doc"):
        cols = jnp.stack([vision[0, 0, :, i * slice_w : (i + 1) * slice_w] for i in range(n_doc)])
        cols = lax.all_to_all(cols, "doc", split_axis=0, concat_axis=0, tiled=True)
        cols = cols.reshape(n_doc * rows32, slice_w)
    with jax.named_scope("vision_tensor"):
        x = lax.all_gather(cols, "tensor", axis=0, tiled=True)

    wrows = w_key.shape[0]
    w = jnp.concatenate([w_key, w_value], axis=1)
    extra = jnp.broadcast_to(image_len.astype(BF), (8, w.shape[1]))
    packed = jnp.concatenate([w, extra], axis=0)
    groups = [[2 * (2 * j + o) + c for j in range(n_z // 2)] for o in range(2) for c in range(2)]
    with jax.named_scope("weights_z"):
        near = lax.all_gather(packed, "seq", axis=0, tiled=False, axis_index_groups=groups)
    with jax.named_scope("weights_pair"):
        beside = lax.ppermute(near, "seq", [(i, i ^ 2) for i in range(n_seq)])
    own = jnp.concatenate([near, beside], axis=0)
    with jax.named_scope("weights_core"):
        other = lax.ppermute(own, "seq", swap)
    with jax.named_scope("project"):
        part = projection(jnp.stack([core, z % 2]), x, own, other)
    with jax.named_scope("reduce_doc"):
        part = part.reshape(-1, n_doc, rows32, w.shape[1])
        part = lax.all_to_all(part, "doc", split_axis=1, concat_axis=1, tiled=True)
        kv = jnp.sum(part, axis=1).reshape(-1, w.shape[1])
    kv = jnp.concatenate([head_norm(kv[:, :HD]), kv[:, HD:]], axis=1).astype(BF)

    def from_chip(block, d):
        return lax.ppermute(block, "seq", chip_shift(n_seq, -d))

    kv = kv[None]
    with jax.named_scope("kv_far"):
        p9, m9 = from_chip(kv, 9), from_chip(kv, -9)
    with jax.named_scope("kv_mid"):
        three = jnp.concatenate([kv, p9, m9], axis=0)
        p15, m15 = from_chip(p9, 6), from_chip(m9, -6)
        p3, m3 = from_chip(three, 3), from_chip(three, -3)
    early = jnp.concatenate([three, p3, m3, p15, m15], axis=0)
    offsets = [0, 9, -9, 3, 12, -6, -3, 6, -12, 15, -15]
    with jax.named_scope("kv_near"):
        up, down = from_chip(early, 1), from_chip(early[:-1], -1)
    late = jnp.concatenate([up, down], axis=0)
    places = [*offsets, *(o + 1 for o in offsets), *(o - 1 for o in offsets[:-1])]
    places = np.array([o % n_z for o in places], np.int32)
    with jax.named_scope("kv_core"):
        early_other = lax.ppermute(early, "seq", swap)
        late_other = lax.ppermute(late, "seq", swap)

    owners = jnp.arange(n_seq, dtype=jnp.int32)
    oz, oc = owners // 2, owners % 2
    here = (oz - z) % n_z
    pair = jnp.sum(jnp.where(here[:, None] == places[None, :], jnp.arange(n_z)[None, :], 0), axis=1)
    pos = 2 * pair + (oc != core).astype(jnp.int32)
    at = owners[:, None] == pos[None, :]
    lens = jnp.concatenate([own[:, wrows, 0], other[:, wrows, 0]]).astype(jnp.int32)
    from_w = n_z * (oc != core).astype(jnp.int32) + (n_z // 2) * ((oz - z) % 2) + oz // 2
    lens = jnp.sum(jnp.where(from_w[:, None] == owners[None, :], lens[None, :], 0), axis=1)
    lens_at = jnp.sum(jnp.where(at, lens[None, :], 0), axis=1)

    image_ids = token_image[0, :, 0]
    owner_pos = jnp.sum(
        jnp.where(image_owner[0][:, None] == owners[None, :], pos[None, :], 0), axis=1
    )
    picked = image_ids[:, None] == owners[None, :]
    target = jnp.sum(jnp.where(picked, owner_pos[None, :], 0), axis=1)
    onehot = (target[:, None] == owners[None, :]).astype(jnp.int32)
    ranks = jnp.cumsum(onehot, axis=0) - onehot
    slot = target * CAP + jnp.sum(ranks * onehot, axis=1)
    dispatch = (slot[:, None] == jnp.arange(n_seq * CAP, dtype=jnp.int32)[None, :]).astype(BF)
    with jax.named_scope("dispatch"):
        q = jnp.dot(dispatch.T, queries[0], preferred_element_type=F32).astype(BF)
    cut = early.shape[0] * 2
    with jax.named_scope("attention_early"):
        first = attention(lens_at[:cut], attn_gate, q[: cut * CAP], early, early_other)
        out = jnp.dot(dispatch[:, : cut * CAP], first, preferred_element_type=F32)
    with jax.named_scope("attention_late"):
        last = attention(lens_at[cut:], attn_gate, q[cut * CAP :], late, late_other)
        out = out + jnp.dot(dispatch[:, cut * CAP :], last, preferred_element_type=F32)
    return out.astype(BF)[None]


def solution(mesh):
    placed = (
        P("doc", "seq", "tensor"),
        P("doc", "seq", "tensor", None),
        P(("doc", "seq"), "tensor"),
        P(("doc", "seq"), "tensor"),
        P(),
        P("doc", "seq", None),
        P("doc", None),
        P("doc", "seq"),
    )
    return jax.shard_map(
        shards, mesh=mesh, in_specs=placed, out_specs=P("doc", "seq", "tensor"), check_vma=False
    )
```

```python
import jax
import jax.numpy as jnp
from jax import lax
from jax.experimental import pallas as pl
from jax.experimental.pallas import tpu as pltpu
from jax.sharding import PartitionSpec as P

HD = 128
CAP = 8
BF = jnp.bfloat16
F32 = jnp.float32
HF = jnp.float16
NOTES = 16
KEY_SCALE = 2048.0
TOP_LEVEL = 14.0


def head_norm(x):
    return x * lax.rsqrt(jnp.mean(x * x, axis=-1, keepdims=True) + 1e-06)


def project(place_ref, x_ref, own_ref, other_ref, out_ref, w_ref):
    rows = w_ref.shape[0] // (own_ref.shape[0] * 2)
    half = own_ref.shape[0] // 2
    core, odd = place_ref[0], place_ref[1]
    for k, ref in enumerate((own_ref, other_ref)):
        for o in range(2):
            for j in range(half):
                owner = 2 * (2 * j + (o + odd) % 2) + (k + core) % 2
                at = pl.ds(pl.multiple_of(owner * rows, rows), rows)
                w_ref[at] = ref[o * half + j]
    out_ref[...] = jnp.dot(x_ref[...], w_ref[...], preferred_element_type=F32)


def projection(place, x, own, other):
    cols = own.shape[2]
    return pl.pallas_call(
        project,
        out_shape=jax.ShapeDtypeStruct((x.shape[0], cols), F32),
        in_specs=[pl.BlockSpec(memory_space=pltpu.SMEM)]
        + [pl.BlockSpec(memory_space=pltpu.VMEM)] * 3,
        out_specs=pl.BlockSpec(memory_space=pltpu.VMEM),
        scratch_shapes=[pltpu.VMEM((x.shape[1], cols), BF)],
        compiler_params=pltpu.CompilerParams(vmem_limit_bytes=32 * 1024 * 1024),
    )(place, x, own, other)


UNROLL = 4


def attend(gate_ref, q_ref, kv_ref, out_ref):
    heads = q_ref.shape[1] // HD
    vtok = kv_ref.shape[1] - NOTES
    pairs = kv_ref.shape[0] // 2
    factor = jnp.tanh(jnp.full((1, 1), gate_ref[0], F32))
    key = lax.broadcasted_iota(jnp.int32, (1, vtok), 1).astype(F32)
    four = (heads, 2, CAP, HD)

    def one(i):
        rows = pl.ds(pl.multiple_of(i * 2 * CAP, 2 * CAP), 2 * CAP)
        q = jnp.concatenate([q_ref[rows, h * HD : (h + 1) * HD] for h in range(heads)], axis=0)
        kv = kv_ref[pl.ds(2 * i, 2), :vtok].reshape(2 * vtok, 2 * HD)
        k, v = kv[:, :HD], kv[:, HD:]
        note = [kv_ref[2 * i + e, vtok:].astype(F32)[:1] for e in range(2)]
        s = lax.dot_general(q, k, (((1,), (1,)), ((), ())), preferred_element_type=F32)
        s = s.reshape(heads, 2, CAP, 2 * vtok) * (HD ** -0.5 / KEY_SCALE)
        s = [
            jnp.where((key < note[e][:, :HD])[None], s[:, e, :, e * vtok : (e + 1) * vtok], -jnp.inf)
            for e in range(2)
        ]
        s = jnp.stack(s, axis=1)
        top = jnp.max(s, axis=-1, keepdims=True)
        p = jnp.exp(s - top)
        total = jnp.sum(p, axis=-1, keepdims=True)
        zero = jnp.zeros_like(p[:, 0])
        left = jnp.stack([p[:, 0], zero], axis=1).reshape(-1, vtok)
        right = jnp.stack([zero, p[:, 1]], axis=1).reshape(-1, vtok)
        p = jnp.concatenate([left, right], axis=1).astype(BF)
        mixed = jnp.dot(p, v, preferred_element_type=F32)
        level = jnp.exp2(jnp.stack([n[:, HD:] for n in note])[None] - TOP_LEVEL)
        ans = mixed.reshape(four) * (factor / total) * level
        ans = ans.reshape(-1, HD).astype(BF)
        for h in range(heads):
            out_ref[rows, h * HD : (h + 1) * HD] = ans[h * 2 * CAP : (h + 1) * 2 * CAP]

    def body(i, carry):
        for u in range(UNROLL):
            one(i * UNROLL + u)
        return carry

    lax.fori_loop(0, pairs // UNROLL, body, 0)


def attention(gate, q, kv):
    smem = pl.BlockSpec(memory_space=pltpu.SMEM)
    vmem = pl.BlockSpec(memory_space=pltpu.VMEM)
    scores = q.size // HD * 2 * kv.shape[1]
    return pl.pallas_call(
        attend,
        out_shape=jax.ShapeDtypeStruct(q.shape, BF),
        in_specs=[smem, vmem, vmem],
        out_specs=vmem,
        cost_estimate=pl.CostEstimate(
            flops=4 * scores * HD, bytes_accessed=2 * kv.size, transcendentals=scores
        ),
        compiler_params=pltpu.CompilerParams(vmem_limit_bytes=32 * 1024 * 1024),
    )(gate, q, kv)


def shards(queries, vision, w_key, w_value, attn_gate, token_image, image_owner, image_len):
    n_doc = lax.axis_size("doc")
    n_seq = lax.axis_size("seq")
    n_z = n_seq // 2
    seq = lax.axis_index("seq")
    core = seq % 2
    z = seq // 2
    rows32, width = vision.shape[2], vision.shape[3]
    slice_w = width // n_doc
    swap = [(i, i ^ 1) for i in range(n_seq)]

    with jax.named_scope("vision_doc"):
        cols = jnp.stack([vision[0, 0, :, i * slice_w : (i + 1) * slice_w] for i in range(n_doc)])
        cols = lax.all_to_all(cols, "doc", split_axis=0, concat_axis=0, tiled=True)
        cols = cols.reshape(n_doc * rows32, slice_w)
    with jax.named_scope("vision_tensor"):
        x = lax.all_gather(cols, "tensor", axis=0, tiled=True)

    owners = jnp.arange(n_seq, dtype=jnp.int32)
    image_ids = token_image[0, :, 0]
    picked = image_ids[:, None] == owners[None, :]
    target = jnp.sum(jnp.where(picked, image_owner[0][None, :], 0), axis=1)
    onehot = (target[:, None] == owners[None, :]).astype(jnp.int32)
    ranks = jnp.cumsum(onehot, axis=0) - onehot
    slot = target * CAP + jnp.sum(ranks * onehot, axis=1)
    dispatch = (slot[:, None] == jnp.arange(n_seq * CAP, dtype=jnp.int32)[None, :]).astype(BF)
    with jax.named_scope("dispatch"):
        q = jnp.dot(dispatch.T, queries[0], preferred_element_type=F32).astype(BF)

    w = jnp.concatenate([w_key, w_value], axis=1)
    groups = [[2 * (2 * j + o) + c for j in range(n_z // 2)] for o in range(2) for c in range(2)]
    with jax.named_scope("weights_z"):
        near = lax.all_gather(w, "seq", axis=0, tiled=False, axis_index_groups=groups)
    with jax.named_scope("weights_pair"):
        beside = lax.ppermute(near, "seq", [(i, i ^ 2) for i in range(n_seq)])
    own = jnp.concatenate([near, beside], axis=0)
    with jax.named_scope("weights_core"):
        other = lax.ppermute(own, "seq", swap)
    own, other, q = lax.optimization_barrier((own, other, q))
    with jax.named_scope("project"):
        part = projection(jnp.stack([core, z % 2]), x, own, other)
    with jax.named_scope("reduce_doc"):
        part = part.reshape(-1, n_doc, rows32, w.shape[1])
        part = lax.all_to_all(part, "doc", split_axis=1, concat_axis=1, tiled=True)
        kv = jnp.sum(part, axis=1).reshape(-1, w.shape[1])
    keys = lax.reduce_precision(head_norm(kv[:, :HD]), 8, 7)
    values = lax.reduce_precision(kv[:, HD:], 8, 7)

    with jax.named_scope("kv_seq"):
        largest = jnp.max(jnp.abs(values), keepdims=True)
        level = jnp.ceil(jnp.log2(jnp.maximum(largest, 1e-30)))
        block = jnp.concatenate([keys * KEY_SCALE, values * jnp.exp2(TOP_LEVEL - level)], axis=1)
        lane = lax.broadcasted_iota(jnp.int32, (NOTES, 2 * HD), 1)
        notes = jnp.where(lane < HD, image_len.astype(F32), level)
        block = jnp.concatenate([block, notes], axis=0).astype(HF)
        blocks = lax.all_gather(block, "seq", axis=0, tiled=False)
    with jax.named_scope("attention"):
        answer = attention(attn_gate, q, blocks.astype(BF))
    with jax.named_scope("combine"):
        out = jnp.dot(dispatch, answer, preferred_element_type=F32)
    return out.astype(BF)[None]


def solution(mesh):
    placed = (
        P("doc", "seq", "tensor"),
        P("doc", "seq", "tensor", None),
        P(("doc", "seq"), "tensor"),
        P(("doc", "seq"), "tensor"),
        P(),
        P("doc", "seq", None),
        P("doc", None),
        P("doc", "seq"),
    )
    return jax.shard_map(
        shards, mesh=mesh, in_specs=placed, out_specs=P("doc", "seq", "tensor"), check_vma=False
    )
```

```python
import jax
import jax.numpy as jnp
from jax import lax
from jax.experimental import pallas as pl
from jax.experimental.pallas import tpu as pltpu
from jax.sharding import PartitionSpec as P

HD = 128
CAP = 8
BF = jnp.bfloat16
F32 = jnp.float32
HF = jnp.float16
NOTES = 16
KEY_SCALE = 2048.0
TOP_LEVEL = 14.0


def head_norm(x):
    return x * lax.rsqrt(jnp.mean(x * x, axis=-1, keepdims=True) + 1e-06)


def project(place_ref, *refs):
    *x_refs, own_ref, other_ref, out_ref, w_ref = refs
    rows = w_ref.shape[0] // (own_ref.shape[0] * 2)
    half = own_ref.shape[0] // 2
    core, odd, tensor = place_ref[0], place_ref[1], place_ref[2]
    for k, ref in enumerate((own_ref, other_ref)):
        for o in range(2):
            for j in range(half):
                owner = 2 * (2 * j + (o + odd) % 2) + (k + core) % 2
                at = pl.ds(pl.multiple_of(owner * rows, rows), rows)
                w_ref[at] = ref[o * half + j]
    x = jnp.concatenate([ref[...] for ref in x_refs], axis=0)
    part = jnp.dot(x, w_ref[...], preferred_element_type=F32)
    n, n_doc = len(x_refs), out_ref.shape[0]
    each = x.shape[0] // (n * n_doc)
    for k in range(n):
        source = (tensor + n - k) % n
        at = pl.ds(pl.multiple_of(source * each, each), each)
        for d in range(n_doc):
            out_ref[d, at] = part[(k * n_doc + d) * each : (k * n_doc + d + 1) * each]


def projection(place, xs, own, other, n_doc):
    cols, depth = own.shape[2], xs[0].shape[1]
    vmem = pl.BlockSpec(memory_space=pltpu.VMEM)
    return pl.pallas_call(
        project,
        out_shape=jax.ShapeDtypeStruct((n_doc, len(xs) * xs[0].shape[0] // n_doc, cols), F32),
        in_specs=[pl.BlockSpec(memory_space=pltpu.SMEM)] + [vmem] * (len(xs) + 2),
        out_specs=vmem,
        scratch_shapes=[pltpu.VMEM((depth, cols), BF)],
        compiler_params=pltpu.CompilerParams(vmem_limit_bytes=32 * 1024 * 1024),
    )(place, *xs, own, other)


UNROLL = 4


def attend(gate_ref, q_ref, kv_ref, out_ref):
    heads = q_ref.shape[1] // HD
    vtok = kv_ref.shape[1] - NOTES
    pairs = kv_ref.shape[0] // 2
    factor = jnp.tanh(jnp.full((1, 1), gate_ref[0], F32))
    key = lax.broadcasted_iota(jnp.int32, (1, vtok), 1).astype(F32)
    four = (heads, 2, CAP, HD)

    def one(i):
        rows = pl.ds(pl.multiple_of(i * 2 * CAP, 2 * CAP), 2 * CAP)
        q = jnp.concatenate([q_ref[rows, h * HD : (h + 1) * HD] for h in range(heads)], axis=0)
        kv = kv_ref[pl.ds(2 * i, 2), :vtok].reshape(2 * vtok, 2 * HD)
        k, v = kv[:, :HD], kv[:, HD:]
        note = [kv_ref[2 * i + e, vtok:].astype(F32)[:1] for e in range(2)]
        s = lax.dot_general(q, k, (((1,), (1,)), ((), ())), preferred_element_type=F32)
        s = s.reshape(heads, 2, CAP, 2 * vtok) * (HD ** -0.5 / KEY_SCALE)
        s = [
            jnp.where((key < note[e][:, :HD])[None], s[:, e, :, e * vtok : (e + 1) * vtok], -jnp.inf)
            for e in range(2)
        ]
        s = jnp.stack(s, axis=1)
        top = jnp.max(s, axis=-1, keepdims=True)
        p = jnp.exp(s - top)
        total = jnp.sum(p, axis=-1, keepdims=True)
        zero = jnp.zeros_like(p[:, 0])
        left = jnp.stack([p[:, 0], zero], axis=1).reshape(-1, vtok)
        right = jnp.stack([zero, p[:, 1]], axis=1).reshape(-1, vtok)
        p = jnp.concatenate([left, right], axis=1).astype(BF)
        mixed = jnp.dot(p, v, preferred_element_type=F32)
        level = jnp.exp2(jnp.stack([n[:, HD:] for n in note])[None] - TOP_LEVEL)
        ans = mixed.reshape(four) * (factor / total) * level
        ans = ans.reshape(-1, HD).astype(BF)
        for h in range(heads):
            out_ref[rows, h * HD : (h + 1) * HD] = ans[h * 2 * CAP : (h + 1) * 2 * CAP]

    def body(i, carry):
        for u in range(UNROLL):
            one(i * UNROLL + u)
        return carry

    lax.fori_loop(0, pairs // UNROLL, body, 0)


def attention(gate, q, kv):
    smem = pl.BlockSpec(memory_space=pltpu.SMEM)
    vmem = pl.BlockSpec(memory_space=pltpu.VMEM)
    scores = q.size // HD * 2 * kv.shape[1]
    return pl.pallas_call(
        attend,
        out_shape=jax.ShapeDtypeStruct(q.shape, BF),
        in_specs=[smem, vmem, vmem],
        out_specs=vmem,
        cost_estimate=pl.CostEstimate(
            flops=4 * scores * HD, bytes_accessed=2 * kv.size, transcendentals=scores
        ),
        compiler_params=pltpu.CompilerParams(vmem_limit_bytes=32 * 1024 * 1024),
    )(gate, q, kv)


def shards(queries, vision, w_key, w_value, attn_gate, token_image, image_owner, image_len):
    n_doc = lax.axis_size("doc")
    n_seq = lax.axis_size("seq")
    n_z = n_seq // 2
    seq = lax.axis_index("seq")
    core = seq % 2
    z = seq // 2
    rows32, width = vision.shape[2], vision.shape[3]
    slice_w = width // n_doc
    swap = [(i, i ^ 1) for i in range(n_seq)]

    with jax.named_scope("vision_doc"):
        cols = jnp.stack([vision[0, 0, :, i * slice_w : (i + 1) * slice_w] for i in range(n_doc)])
        cols = lax.all_to_all(cols, "doc", split_axis=0, concat_axis=0, tiled=True)
        cols = cols.reshape(n_doc * rows32, slice_w)
    w = jnp.concatenate([w_key, w_value], axis=1)
    cols, w = lax.optimization_barrier((cols, w))
    n_tensor = lax.axis_size("tensor")
    with jax.named_scope("vision_tensor"):
        xs = [cols] + [
            lax.ppermute(cols, "tensor", [(i, (i + k) % n_tensor) for i in range(n_tensor)])
            for k in range(1, n_tensor)
        ]

    groups = [[2 * (2 * j + o) + c for j in range(n_z // 2)] for o in range(2) for c in range(2)]
    with jax.named_scope("weights_z"):
        near = lax.all_gather(w, "seq", axis=0, tiled=False, axis_index_groups=groups)
    near, token_image, *xs = lax.optimization_barrier((near, token_image, *xs))
    owners = jnp.arange(n_seq, dtype=jnp.int32)
    image_ids = token_image[0, :, 0]
    picked = image_ids[:, None] == owners[None, :]
    target = jnp.sum(jnp.where(picked, image_owner[0][None, :], 0), axis=1)
    onehot = (target[:, None] == owners[None, :]).astype(jnp.int32)
    ranks = jnp.cumsum(onehot, axis=0) - onehot
    slot = target * CAP + jnp.sum(ranks * onehot, axis=1)
    dispatch = (slot[:, None] == jnp.arange(n_seq * CAP, dtype=jnp.int32)[None, :]).astype(BF)
    with jax.named_scope("dispatch"):
        q = jnp.dot(dispatch.T, queries[0], preferred_element_type=F32).astype(BF)

    with jax.named_scope("weights_pair"):
        beside = lax.ppermute(near, "seq", [(i, i ^ 2) for i in range(n_seq)])
    own = jnp.concatenate([near, beside], axis=0)
    with jax.named_scope("weights_core"):
        other = lax.ppermute(own, "seq", swap)
    own, other, q = lax.optimization_barrier((own, other, q))
    with jax.named_scope("project"):
        place = jnp.stack([core, z % 2, lax.axis_index("tensor")])
        part = projection(place, xs, own, other, n_doc)
    with jax.named_scope("reduce_doc"):
        part = lax.all_to_all(part, "doc", split_axis=0, concat_axis=0, tiled=True)
        kv = jnp.sum(part, axis=0)
    keys = lax.reduce_precision(head_norm(kv[:, :HD]), 8, 7)
    values = lax.reduce_precision(kv[:, HD:], 8, 7)

    with jax.named_scope("kv_seq"):
        largest = jnp.max(jnp.abs(values), keepdims=True)
        level = jnp.ceil(jnp.log2(jnp.maximum(largest, 1e-30)))
        block = jnp.concatenate([keys * KEY_SCALE, values * jnp.exp2(TOP_LEVEL - level)], axis=1)
        lane = lax.broadcasted_iota(jnp.int32, (NOTES, 2 * HD), 1)
        notes = jnp.where(lane < HD, image_len.astype(F32), level)
        block = jnp.concatenate([block, notes], axis=0).astype(HF)
        blocks = lax.all_gather(block, "seq", axis=0, tiled=False)
    with jax.named_scope("attention"):
        answer = attention(attn_gate, q, blocks.astype(BF))
    with jax.named_scope("combine"):
        out = jnp.dot(dispatch, answer, preferred_element_type=F32)
    return out.astype(BF)[None]


def solution(mesh):
    placed = (
        P("doc", "seq", "tensor"),
        P("doc", "seq", "tensor", None),
        P(("doc", "seq"), "tensor"),
        P(("doc", "seq"), "tensor"),
        P(),
        P("doc", "seq", None),
        P("doc", None),
        P("doc", "seq"),
    )
    return jax.shard_map(
        shards, mesh=mesh, in_specs=placed, out_specs=P("doc", "seq", "tensor"), check_vma=False
    )
```

```python
import jax
import jax.numpy as jnp
from jax import lax
from jax.experimental import pallas as pl
from jax.experimental.pallas import tpu as pltpu
from jax.sharding import PartitionSpec as P

HD = 128
CAP = 8
BF = jnp.bfloat16
F32 = jnp.float32
HF = jnp.float16
NOTES = 16
KEY_SCALE = 2048.0
TOP_LEVEL = 14.0


def head_norm(x):
    return x * lax.rsqrt(jnp.mean(x * x, axis=-1, keepdims=True) + 1e-06)


def spread(v_ref, out_ref):
    n_doc, copies, _, width = out_ref.shape
    for d in range(n_doc):
        part = v_ref[:, d * width : (d + 1) * width]
        for t in range(copies):
            out_ref[d, t] = part


def spreading(v, n_doc, copies):
    vmem = pl.BlockSpec(memory_space=pltpu.VMEM)
    shape = (n_doc, copies, v.shape[0], v.shape[1] // n_doc)
    return pl.pallas_call(
        spread,
        out_shape=jax.ShapeDtypeStruct(shape, v.dtype),
        in_specs=[vmem],
        out_specs=vmem,
        compiler_params=pltpu.CompilerParams(vmem_limit_bytes=32 * 1024 * 1024),
    )(v)


def project(place_ref, x_ref, own_ref, other_ref, out_ref, w_ref):
    rows = w_ref.shape[0] // (own_ref.shape[0] * 2)
    half = own_ref.shape[0] // 2
    core, odd = place_ref[0], place_ref[1]
    for k, ref in enumerate((own_ref, other_ref)):
        for o in range(2):
            for j in range(half):
                owner = 2 * (2 * j + (o + odd) % 2) + (k + core) % 2
                at = pl.ds(pl.multiple_of(owner * rows, rows), rows)
                w_ref[at] = ref[o * half + j]
    out_ref[...] = jnp.dot(x_ref[...], w_ref[...], preferred_element_type=F32)


def projection(place, x, own, other):
    cols = own.shape[2]
    vmem = pl.BlockSpec(memory_space=pltpu.VMEM)
    return pl.pallas_call(
        project,
        out_shape=jax.ShapeDtypeStruct((x.shape[0], cols), F32),
        in_specs=[pl.BlockSpec(memory_space=pltpu.SMEM), vmem, vmem, vmem],
        out_specs=vmem,
        scratch_shapes=[pltpu.VMEM((x.shape[1], cols), BF)],
        compiler_params=pltpu.CompilerParams(vmem_limit_bytes=32 * 1024 * 1024),
    )(place, x, own, other)


UNROLL = 4


def attend(gate_ref, q_ref, kv_ref, out_ref):
    heads = q_ref.shape[1] // HD
    vtok = kv_ref.shape[1] - NOTES
    pairs = kv_ref.shape[0] // 2
    factor = jnp.tanh(jnp.full((1, 1), gate_ref[0], F32))
    key = lax.broadcasted_iota(jnp.int32, (1, vtok), 1).astype(F32)
    four = (heads, 2, CAP, HD)

    def one(i):
        rows = pl.ds(pl.multiple_of(i * 2 * CAP, 2 * CAP), 2 * CAP)
        q = jnp.concatenate([q_ref[rows, h * HD : (h + 1) * HD] for h in range(heads)], axis=0)
        kv = kv_ref[pl.ds(2 * i, 2), :vtok].reshape(2 * vtok, 2 * HD)
        k, v = kv[:, :HD], kv[:, HD:]
        note = [kv_ref[2 * i + e, vtok:].astype(F32)[:1] for e in range(2)]
        s = lax.dot_general(q, k, (((1,), (1,)), ((), ())), preferred_element_type=F32)
        s = s.reshape(heads, 2, CAP, 2 * vtok) * (HD ** -0.5 / KEY_SCALE)
        s = [
            jnp.where((key < note[e][:, :HD])[None], s[:, e, :, e * vtok : (e + 1) * vtok], -jnp.inf)
            for e in range(2)
        ]
        s = jnp.stack(s, axis=1)
        top = jnp.max(s, axis=-1, keepdims=True)
        p = jnp.exp(s - top)
        total = jnp.sum(p, axis=-1, keepdims=True)
        zero = jnp.zeros_like(p[:, 0])
        left = jnp.stack([p[:, 0], zero], axis=1).reshape(-1, vtok)
        right = jnp.stack([zero, p[:, 1]], axis=1).reshape(-1, vtok)
        p = jnp.concatenate([left, right], axis=1).astype(BF)
        mixed = jnp.dot(p, v, preferred_element_type=F32)
        level = jnp.exp2(jnp.stack([n[:, HD:] for n in note])[None] - TOP_LEVEL)
        ans = mixed.reshape(four) * (factor / total) * level
        ans = ans.reshape(-1, HD).astype(BF)
        for h in range(heads):
            out_ref[rows, h * HD : (h + 1) * HD] = ans[h * 2 * CAP : (h + 1) * 2 * CAP]

    def body(i, carry):
        for u in range(UNROLL):
            one(i * UNROLL + u)
        return carry

    lax.fori_loop(0, pairs // UNROLL, body, 0)


def attention(gate, q, kv):
    smem = pl.BlockSpec(memory_space=pltpu.SMEM)
    vmem = pl.BlockSpec(memory_space=pltpu.VMEM)
    scores = q.size // HD * 2 * kv.shape[1]
    return pl.pallas_call(
        attend,
        out_shape=jax.ShapeDtypeStruct(q.shape, BF),
        in_specs=[smem, vmem, vmem],
        out_specs=vmem,
        cost_estimate=pl.CostEstimate(
            flops=4 * scores * HD, bytes_accessed=2 * kv.size, transcendentals=scores
        ),
        compiler_params=pltpu.CompilerParams(vmem_limit_bytes=32 * 1024 * 1024),
    )(gate, q, kv)


def shards(queries, vision, w_key, w_value, attn_gate, token_image, image_owner, image_len):
    n_doc = lax.axis_size("doc")
    n_seq = lax.axis_size("seq")
    n_z = n_seq // 2
    seq = lax.axis_index("seq")
    core = seq % 2
    z = seq // 2
    rows32, width = vision.shape[2], vision.shape[3]
    slice_w = width // n_doc
    swap = [(i, i ^ 1) for i in range(n_seq)]

    n_tensor = lax.axis_size("tensor")
    w = jnp.concatenate([w_key, w_value], axis=1)
    with jax.named_scope("vision_doc_tensor"):
        x = spreading(vision[0, 0], n_doc, n_tensor).reshape(-1, rows32, slice_w)
        x = lax.all_to_all(x, ("doc", "tensor"), split_axis=0, concat_axis=0, tiled=True)
        x = x.reshape(-1, slice_w)

    groups = [[2 * (2 * j + o) + c for j in range(n_z // 2)] for o in range(2) for c in range(2)]
    with jax.named_scope("weights_z"):
        near = lax.all_gather(w, "seq", axis=0, tiled=False, axis_index_groups=groups)
    near, token_image, x = lax.optimization_barrier((near, token_image, x))
    owners = jnp.arange(n_seq, dtype=jnp.int32)
    image_ids = token_image[0, :, 0]
    picked = image_ids[:, None] == owners[None, :]
    target = jnp.sum(jnp.where(picked, image_owner[0][None, :], 0), axis=1)
    onehot = (target[:, None] == owners[None, :]).astype(jnp.int32)
    ranks = jnp.cumsum(onehot, axis=0) - onehot
    slot = target * CAP + jnp.sum(ranks * onehot, axis=1)
    dispatch = (slot[:, None] == jnp.arange(n_seq * CAP, dtype=jnp.int32)[None, :]).astype(BF)
    with jax.named_scope("dispatch"):
        q = jnp.dot(dispatch.T, queries[0], preferred_element_type=F32).astype(BF)

    with jax.named_scope("weights_pair"):
        beside = lax.ppermute(near, "seq", [(i, i ^ 2) for i in range(n_seq)])
    own = jnp.concatenate([near, beside], axis=0)
    with jax.named_scope("weights_core"):
        other = lax.ppermute(own, "seq", swap)
    own, other, q = lax.optimization_barrier((own, other, q))
    with jax.named_scope("project"):
        part = projection(jnp.stack([core, z % 2]), x, own, other)
    with jax.named_scope("reduce_doc"):
        part = part.reshape(n_doc, -1, w.shape[1])
        part = lax.all_to_all(part, "doc", split_axis=0, concat_axis=0, tiled=True)
        kv = jnp.sum(part, axis=0)
    keys = lax.reduce_precision(head_norm(kv[:, :HD]), 8, 7)
    values = lax.reduce_precision(kv[:, HD:], 8, 7)

    with jax.named_scope("kv_seq"):
        largest = jnp.max(jnp.abs(values), keepdims=True)
        level = jnp.ceil(jnp.log2(jnp.maximum(largest, 1e-30)))
        block = jnp.concatenate([keys * KEY_SCALE, values * jnp.exp2(TOP_LEVEL - level)], axis=1)
        lane = lax.broadcasted_iota(jnp.int32, (NOTES, 2 * HD), 1)
        notes = jnp.where(lane < HD, image_len.astype(F32), level)
        block = jnp.concatenate([block, notes], axis=0).astype(HF)
        blocks = lax.all_gather(block, "seq", axis=0, tiled=False)
    with jax.named_scope("attention"):
        answer = attention(attn_gate, q, blocks.astype(BF))
    with jax.named_scope("combine"):
        out = jnp.dot(dispatch, answer, preferred_element_type=F32)
    return out.astype(BF)[None]


def solution(mesh):
    placed = (
        P("doc", "seq", "tensor"),
        P("doc", "seq", "tensor", None),
        P(("doc", "seq"), "tensor"),
        P(("doc", "seq"), "tensor"),
        P(),
        P("doc", "seq", None),
        P("doc", None),
        P("doc", "seq"),
    )
    return jax.shard_map(
        shards, mesh=mesh, in_specs=placed, out_specs=P("doc", "seq", "tensor"), check_vma=False
    )
```

```python
import jax
import jax.numpy as jnp
from jax import lax
from jax.experimental import pallas as pl
from jax.experimental.pallas import tpu as pltpu
from jax.sharding import PartitionSpec as P

HD = 128
CAP = 8
BF = jnp.bfloat16
F32 = jnp.float32
HF = jnp.float16
NOTES = 16
KEY_SCALE = 2048.0
TOP_LEVEL = 14.0


def head_norm(x):
    return x * lax.rsqrt(jnp.mean(x * x, axis=-1, keepdims=True) + 1e-06)


def spread(v_ref, out_ref):
    n_doc, copies, _, width = out_ref.shape
    for d in range(n_doc):
        part = v_ref[:, d * width : (d + 1) * width]
        for t in range(copies):
            out_ref[d, t] = part


def spreading(v, n_doc, copies):
    vmem = pl.BlockSpec(memory_space=pltpu.VMEM)
    shape = (n_doc, copies, v.shape[0], v.shape[1] // n_doc)
    return pl.pallas_call(
        spread,
        out_shape=jax.ShapeDtypeStruct(shape, v.dtype),
        in_specs=[vmem],
        out_specs=vmem,
        compiler_params=pltpu.CompilerParams(vmem_limit_bytes=32 * 1024 * 1024),
    )(v)


def project(place_ref, x_ref, own_ref, other_ref, out_ref, w_ref):
    rows = w_ref.shape[0] // (own_ref.shape[0] * 2)
    half = own_ref.shape[0] // 2
    core, odd = place_ref[0], place_ref[1]
    for k, ref in enumerate((own_ref, other_ref)):
        for o in range(2):
            for j in range(half):
                owner = 2 * (2 * j + (o + odd) % 2) + (k + core) % 2
                at = pl.ds(pl.multiple_of(owner * rows, rows), rows)
                w_ref[at] = ref[o * half + j]
    out_ref[...] = jnp.dot(x_ref[...], w_ref[...], preferred_element_type=F32)


def projection(place, x, own, other):
    cols = own.shape[2]
    vmem = pl.BlockSpec(memory_space=pltpu.VMEM)
    return pl.pallas_call(
        project,
        out_shape=jax.ShapeDtypeStruct((x.shape[0], cols), F32),
        in_specs=[pl.BlockSpec(memory_space=pltpu.SMEM), vmem, vmem, vmem],
        out_specs=vmem,
        scratch_shapes=[pltpu.VMEM((x.shape[1], cols), BF)],
        compiler_params=pltpu.CompilerParams(vmem_limit_bytes=32 * 1024 * 1024),
    )(place, x, own, other)


UNROLL = 4


def attend(gate_ref, q_ref, kv_ref, out_ref):
    heads = q_ref.shape[1] // HD
    vtok = kv_ref.shape[1] - NOTES
    pairs = kv_ref.shape[0] // 2
    factor = jnp.tanh(jnp.full((1, 1), gate_ref[0], F32))
    key = lax.broadcasted_iota(jnp.int32, (1, vtok), 1).astype(F32)
    four = (heads, 2, CAP, HD)

    def one(i):
        rows = pl.ds(pl.multiple_of(i * 2 * CAP, 2 * CAP), 2 * CAP)
        q = jnp.concatenate([q_ref[rows, h * HD : (h + 1) * HD] for h in range(heads)], axis=0)
        kv = kv_ref[pl.ds(2 * i, 2), :vtok].reshape(2 * vtok, 2 * HD)
        k, v = kv[:, :HD], kv[:, HD:]
        note = [kv_ref[2 * i + e, vtok:].astype(F32)[:1] for e in range(2)]
        s = lax.dot_general(q, k, (((1,), (1,)), ((), ())), preferred_element_type=F32)
        s = s.reshape(heads, 2, CAP, 2 * vtok) * (HD ** -0.5 / KEY_SCALE)
        s = [
            jnp.where((key < note[e][:, :HD])[None], s[:, e, :, e * vtok : (e + 1) * vtok], -jnp.inf)
            for e in range(2)
        ]
        s = jnp.stack(s, axis=1)
        top = jnp.max(s, axis=-1, keepdims=True)
        p = jnp.exp(s - top)
        total = jnp.sum(p, axis=-1, keepdims=True)
        zero = jnp.zeros_like(p[:, 0])
        left = jnp.stack([p[:, 0], zero], axis=1).reshape(-1, vtok)
        right = jnp.stack([zero, p[:, 1]], axis=1).reshape(-1, vtok)
        p = jnp.concatenate([left, right], axis=1).astype(BF)
        mixed = jnp.dot(p, v, preferred_element_type=F32)
        level = jnp.exp2(jnp.stack([n[:, HD:] for n in note])[None] - TOP_LEVEL)
        ans = mixed.reshape(four) * (factor / total) * level
        ans = ans.reshape(-1, HD).astype(BF)
        for h in range(heads):
            out_ref[rows, h * HD : (h + 1) * HD] = ans[h * 2 * CAP : (h + 1) * 2 * CAP]

    def body(i, carry):
        for u in range(UNROLL):
            one(i * UNROLL + u)
        return carry

    lax.fori_loop(0, pairs // UNROLL, body, 0)


def attention(gate, q, kv):
    smem = pl.BlockSpec(memory_space=pltpu.SMEM)
    vmem = pl.BlockSpec(memory_space=pltpu.VMEM)
    scores = q.size // HD * 2 * kv.shape[1]
    return pl.pallas_call(
        attend,
        out_shape=jax.ShapeDtypeStruct(q.shape, BF),
        in_specs=[smem, vmem, vmem],
        out_specs=vmem,
        cost_estimate=pl.CostEstimate(
            flops=4 * scores * HD, bytes_accessed=2 * kv.size, transcendentals=scores
        ),
        compiler_params=pltpu.CompilerParams(vmem_limit_bytes=32 * 1024 * 1024),
    )(gate, q, kv)


def shards(queries, vision, w_key, w_value, attn_gate, token_image, image_owner, image_len):
    n_doc = lax.axis_size("doc")
    n_seq = lax.axis_size("seq")
    n_z = n_seq // 2
    seq = lax.axis_index("seq")
    core = seq % 2
    z = seq // 2
    rows32, width = vision.shape[2], vision.shape[3]
    slice_w = width // n_doc
    swap = [(i, i ^ 1) for i in range(n_seq)]

    n_tensor = lax.axis_size("tensor")
    w = jnp.concatenate([w_key, w_value], axis=1)
    with jax.named_scope("vision_doc_tensor"):
        x = spreading(vision[0, 0], n_doc, n_tensor).reshape(-1, rows32, slice_w)
        x = lax.all_to_all(x, ("doc", "tensor"), split_axis=0, concat_axis=0, tiled=True)
        x = x.reshape(-1, slice_w)

    groups = [[2 * (2 * j + o) + c for j in range(n_z // 2)] for o in range(2) for c in range(2)]
    with jax.named_scope("weights_z"):
        near = lax.all_gather(w, "seq", axis=0, tiled=False, axis_index_groups=groups)
    near, token_image, x = lax.optimization_barrier((near, token_image, x))
    owners = jnp.arange(n_seq, dtype=jnp.int32)
    image_ids = token_image[0, :, 0]
    picked = image_ids[:, None] == owners[None, :]
    target = jnp.sum(jnp.where(picked, image_owner[0][None, :], 0), axis=1)
    onehot = (target[:, None] == owners[None, :]).astype(jnp.int32)
    ranks = jnp.cumsum(onehot, axis=0) - onehot
    step, odd = target // 4, (target // 2 + z) % 2
    half = n_seq // 8
    later = n_seq // 2 + jnp.where(step // half == core, 0, 2 * half) + 2 * (step % half)
    place = jnp.where(odd == 0, 2 * step, later) + target % 2
    slot = place * CAP + jnp.sum(ranks * onehot, axis=1)
    dispatch = (slot[:, None] == jnp.arange(n_seq * CAP, dtype=jnp.int32)[None, :]).astype(BF)
    with jax.named_scope("dispatch"):
        q = jnp.dot(dispatch.T, queries[0], preferred_element_type=F32).astype(BF)

    with jax.named_scope("weights_pair"):
        beside = lax.ppermute(near, "seq", [(i, i ^ 2) for i in range(n_seq)])
    own = jnp.concatenate([near, beside], axis=0)
    with jax.named_scope("weights_core"):
        other = lax.ppermute(own, "seq", swap)
    own, other, q = lax.optimization_barrier((own, other, q))
    with jax.named_scope("project"):
        part = projection(jnp.stack([core, z % 2]), x, own, other)
    with jax.named_scope("reduce_doc"):
        part = part.reshape(n_doc, -1, w.shape[1])
        part = lax.all_to_all(part, "doc", split_axis=0, concat_axis=0, tiled=True)
        kv = jnp.sum(part, axis=0)
    keys = lax.reduce_precision(head_norm(kv[:, :HD]), 8, 7)
    values = lax.reduce_precision(kv[:, HD:], 8, 7)

    with jax.named_scope("kv_seq"):
        largest = jnp.max(jnp.abs(values), keepdims=True)
        level = jnp.ceil(jnp.log2(jnp.maximum(largest, 1e-30)))
        block = jnp.concatenate([keys * KEY_SCALE, values * jnp.exp2(TOP_LEVEL - level)], axis=1)
        lane = lax.broadcasted_iota(jnp.int32, (NOTES, 2 * HD), 1)
        notes = jnp.where(lane < HD, image_len.astype(F32), level)
        block = jnp.concatenate([block, notes], axis=0).astype(HF)
        groups = [[4 * j + 2 * o + c for j in range(n_z // 2) for c in range(2)] for o in range(2)]
        blocks = lax.all_gather(block, "seq", axis=0, tiled=False, axis_index_groups=groups)
        many = blocks.shape[0] // 2
        give = lax.dynamic_slice_in_dim(blocks, core * many, many, axis=0)
        beside = [(i, (i + (2 if i % 2 else -2)) % n_seq) for i in range(n_seq)]
        fetched = lax.ppermute(give, "seq", beside)
    answers, start = [], 0

    def answer(held):
        size = held.shape[0] * CAP
        return attention(attn_gate, q[start : start + size], held.astype(BF))

    with jax.named_scope("attention_first"):
        first = answer(blocks)
        fetched, first = lax.optimization_barrier((fetched, first))
        answers, start = [first], first.shape[0]
    with jax.named_scope("kv_core"):
        swapped = lax.ppermute(fetched, "seq", swap)
    with jax.named_scope("attention_rest"):
        for held in (fetched, swapped):
            answers.append(answer(held))
            start += answers[-1].shape[0]
    with jax.named_scope("combine"):
        cut = start - answers[-1].shape[0]
        early = jnp.concatenate(answers[:-1], axis=0)
        out = jnp.dot(dispatch[:, :cut], early, preferred_element_type=F32)
        out = out + jnp.dot(dispatch[:, cut:], answers[-1], preferred_element_type=F32)
    return out.astype(BF)[None]


def solution(mesh):
    placed = (
        P("doc", "seq", "tensor"),
        P("doc", "seq", "tensor", None),
        P(("doc", "seq"), "tensor"),
        P(("doc", "seq"), "tensor"),
        P(),
        P("doc", "seq", None),
        P("doc", None),
        P("doc", "seq"),
    )
    return jax.shard_map(
        shards, mesh=mesh, in_specs=placed, out_specs=P("doc", "seq", "tensor"), check_vma=False
    )
```

```python
import jax
import jax.numpy as jnp
from jax import lax
from jax.experimental import pallas as pl
from jax.experimental.pallas import tpu as pltpu
from jax.sharding import PartitionSpec as P

HD = 128
CAP = 8
BF = jnp.bfloat16
F32 = jnp.float32
HF = jnp.float16
NOTES = 8
KEY_SCALE = 2048.0
TOP_LEVEL = 14.0


def head_norm(x):
    return x * lax.rsqrt(jnp.mean(x * x, axis=-1, keepdims=True) + 1e-06)


def spread(v_ref, out_ref):
    n_doc, copies, _, width = out_ref.shape
    for d in range(n_doc):
        part = v_ref[:, d * width : (d + 1) * width]
        for t in range(copies):
            out_ref[d, t] = part


def spreading(v, n_doc, copies):
    vmem = pl.BlockSpec(memory_space=pltpu.VMEM)
    shape = (n_doc, copies, v.shape[0], v.shape[1] // n_doc)
    return pl.pallas_call(
        spread,
        out_shape=jax.ShapeDtypeStruct(shape, v.dtype),
        in_specs=[vmem],
        out_specs=vmem,
        compiler_params=pltpu.CompilerParams(vmem_limit_bytes=32 * 1024 * 1024),
    )(v)


def project(place_ref, x_ref, own_ref, other_ref, out_ref, w_ref):
    rows = w_ref.shape[0] // (own_ref.shape[0] * 2)
    half = own_ref.shape[0] // 2
    core, odd = place_ref[0], place_ref[1]
    for k, ref in enumerate((own_ref, other_ref)):
        for o in range(2):
            for j in range(half):
                owner = 2 * (2 * j + (o + odd) % 2) + (k + core) % 2
                at = pl.ds(pl.multiple_of(owner * rows, rows), rows)
                w_ref[at] = ref[o * half + j]
    out_ref[...] = jnp.dot(x_ref[...], w_ref[...], preferred_element_type=F32)


def projection(place, x, own, other):
    cols = own.shape[2]
    vmem = pl.BlockSpec(memory_space=pltpu.VMEM)
    return pl.pallas_call(
        project,
        out_shape=jax.ShapeDtypeStruct((x.shape[0], cols), F32),
        in_specs=[pl.BlockSpec(memory_space=pltpu.SMEM), vmem, vmem, vmem],
        out_specs=vmem,
        scratch_shapes=[pltpu.VMEM((x.shape[1], cols), BF)],
        compiler_params=pltpu.CompilerParams(vmem_limit_bytes=32 * 1024 * 1024),
    )(place, x, own, other)


def finish(len_ref, part_ref, out_ref):
    kv = part_ref[0]
    for d in range(1, part_ref.shape[0]):
        kv = kv + part_ref[d]
    vtok = kv.shape[0]
    keys = head_norm(kv[:, :HD]).astype(BF).astype(F32)
    values = kv[:, HD:].astype(BF).astype(F32)
    largest = jnp.max(jnp.max(jnp.abs(values), axis=1, keepdims=True), axis=0, keepdims=True)
    level = jnp.ceil(jnp.log2(jnp.maximum(largest, 1e-30)))
    length = jnp.full((NOTES, HD), len_ref[0, 0], jnp.int32).astype(F32)
    out_ref[:vtok, :HD] = keys * KEY_SCALE
    out_ref[:vtok, HD:] = values * jnp.exp2(TOP_LEVEL - level)
    out_ref[vtok:, :HD] = length
    out_ref[vtok:, HD:] = jnp.broadcast_to(level, (NOTES, HD))


def finishing(length, part):
    vmem = pl.BlockSpec(memory_space=pltpu.VMEM)
    return pl.pallas_call(
        finish,
        out_shape=jax.ShapeDtypeStruct((part.shape[1] + NOTES, part.shape[2]), F32),
        in_specs=[pl.BlockSpec(memory_space=pltpu.SMEM), vmem],
        out_specs=vmem,
        compiler_params=pltpu.CompilerParams(vmem_limit_bytes=32 * 1024 * 1024),
    )(length, part)


UNROLL = 8


def attend(gate_ref, q_ref, kv_ref, out_ref):
    heads = q_ref.shape[1] // HD
    vtok = kv_ref.shape[1] - 2 * NOTES
    pairs = kv_ref.shape[0] // 2
    factor = jnp.tanh(jnp.full((1, 1), gate_ref[0], F32))
    key = lax.broadcasted_iota(jnp.int32, (1, vtok), 1).astype(F32)
    four = (heads, 2, CAP, HD)

    def one(i):
        rows = pl.ds(pl.multiple_of(i * 2 * CAP, 2 * CAP), 2 * CAP)
        q = jnp.concatenate([q_ref[rows, h * HD : (h + 1) * HD] for h in range(heads)], axis=0)
        kv = kv_ref[pl.ds(2 * i, 2), :vtok].reshape(2 * vtok, 2 * HD)
        k, v = kv[:, :HD], kv[:, HD:]
        note = [kv_ref[2 * i + e, vtok:].astype(F32)[:1] for e in range(2)]
        s = lax.dot_general(q, k, (((1,), (1,)), ((), ())), preferred_element_type=F32)
        s = s.reshape(heads, 2, CAP, 2 * vtok) * (HD ** -0.5 / KEY_SCALE)
        s = [
            jnp.where((key < note[e][:, :HD])[None], s[:, e, :, e * vtok : (e + 1) * vtok], -jnp.inf)
            for e in range(2)
        ]
        s = jnp.stack(s, axis=1)
        top = jnp.max(s, axis=-1, keepdims=True)
        p = jnp.exp(s - top)
        total = jnp.sum(p, axis=-1, keepdims=True)
        zero = jnp.zeros_like(p[:, 0])
        left = jnp.stack([p[:, 0], zero], axis=1).reshape(-1, vtok)
        right = jnp.stack([zero, p[:, 1]], axis=1).reshape(-1, vtok)
        p = jnp.concatenate([left, right], axis=1).astype(BF)
        mixed = jnp.dot(p, v, preferred_element_type=F32)
        level = jnp.exp2(jnp.stack([n[:, HD:] for n in note])[None] - TOP_LEVEL)
        ans = mixed.reshape(four) * (factor / total) * level
        ans = ans.reshape(-1, HD).astype(BF)
        for h in range(heads):
            out_ref[rows, h * HD : (h + 1) * HD] = ans[h * 2 * CAP : (h + 1) * 2 * CAP]

    def body(i, carry):
        for u in range(unroll):
            one(i * unroll + u)
        return carry

    unroll = min(UNROLL, pairs)
    lax.fori_loop(0, pairs // unroll, body, 0)


def attention(gate, q, kv):
    smem = pl.BlockSpec(memory_space=pltpu.SMEM)
    vmem = pl.BlockSpec(memory_space=pltpu.VMEM)
    scores = q.size // HD * 2 * kv.shape[1]
    return pl.pallas_call(
        attend,
        out_shape=jax.ShapeDtypeStruct(q.shape, BF),
        in_specs=[smem, vmem, vmem],
        out_specs=vmem,
        cost_estimate=pl.CostEstimate(
            flops=4 * scores * HD, bytes_accessed=2 * kv.size, transcendentals=scores
        ),
        compiler_params=pltpu.CompilerParams(vmem_limit_bytes=32 * 1024 * 1024),
    )(gate, q, kv)


def shards(queries, vision, w_key, w_value, attn_gate, token_image, image_owner, image_len):
    n_doc = lax.axis_size("doc")
    n_seq = lax.axis_size("seq")
    n_z = n_seq // 2
    seq = lax.axis_index("seq")
    core = seq % 2
    z = seq // 2
    rows32, width = vision.shape[2], vision.shape[3]
    slice_w = width // n_doc
    swap = [(i, i ^ 1) for i in range(n_seq)]

    n_tensor = lax.axis_size("tensor")
    w = jnp.concatenate([w_key, w_value], axis=1)
    with jax.named_scope("vision_doc_tensor"):
        x = spreading(vision[0, 0], n_doc, n_tensor).reshape(-1, rows32, slice_w)
        x = lax.all_to_all(x, ("doc", "tensor"), split_axis=0, concat_axis=0, tiled=True)
        x = x.reshape(-1, slice_w)

    groups = [[2 * (2 * j + o) + c for j in range(n_z // 2)] for o in range(2) for c in range(2)]
    with jax.named_scope("weights_z"):
        near = lax.all_gather(w, "seq", axis=0, tiled=False, axis_index_groups=groups)
    near, token_image, x = lax.optimization_barrier((near, token_image, x))
    owners = jnp.arange(n_seq, dtype=jnp.int32)
    image_ids = token_image[0, :, 0]
    picked = image_ids[:, None] == owners[None, :]
    target = jnp.sum(jnp.where(picked, image_owner[0][None, :], 0), axis=1)
    onehot = (target[:, None] == owners[None, :]).astype(jnp.int32)
    ranks = jnp.cumsum(onehot, axis=0) - onehot
    step, odd = target // 4, (target // 2 + z) % 2
    half = n_seq // 8
    later = n_seq // 2 + jnp.where(step // half == core, 0, 2 * half) + 2 * (step % half)
    place = jnp.where(odd == 0, 2 * step, later) + target % 2
    slot = place * CAP + jnp.sum(ranks * onehot, axis=1)
    dispatch = (slot[:, None] == jnp.arange(n_seq * CAP, dtype=jnp.int32)[None, :]).astype(BF)
    with jax.named_scope("dispatch"):
        q = jnp.dot(dispatch.T, queries[0], preferred_element_type=F32).astype(BF)

    with jax.named_scope("weights_pair"):
        beside = lax.ppermute(near, "seq", [(i, i ^ 2) for i in range(n_seq)])
    own = jnp.concatenate([near, beside], axis=0)
    with jax.named_scope("weights_core"):
        other = lax.ppermute(own, "seq", swap)
    own, other, q = lax.optimization_barrier((own, other, q))
    with jax.named_scope("project"):
        part = projection(jnp.stack([core, z % 2]), x, own, other)
    with jax.named_scope("reduce_doc"):
        part = part.reshape(n_doc, -1, w.shape[1])
        part = lax.all_to_all(part, "doc", split_axis=0, concat_axis=0, tiled=True)

    with jax.named_scope("kv_seq"):
        block = finishing(image_len, part).astype(HF)
        groups = [[4 * j + 2 * o + c for j in range(n_z // 2) for c in range(2)] for o in range(2)]
        blocks = lax.all_gather(block, "seq", axis=0, tiled=False, axis_index_groups=groups)
        many = blocks.shape[0] // 2
        give = lax.dynamic_slice_in_dim(blocks, core * many, many, axis=0)
        beside = [(i, (i + (2 if i % 2 else -2)) % n_seq) for i in range(n_seq)]
        fetched = lax.ppermute(give, "seq", beside)
    answers, start = [], 0

    def answer(held):
        size = held.shape[0] * CAP
        return attention(attn_gate, q[start : start + size], jnp.pad(held.astype(BF), ((0, 0), (0, NOTES), (0, 0))))

    with jax.named_scope("attention_first"):
        first = answer(blocks)
        fetched, first = lax.optimization_barrier((fetched, first))
        answers, start = [first], first.shape[0]
    with jax.named_scope("kv_core"):
        swapped = lax.ppermute(fetched, "seq", swap)
    with jax.named_scope("attention_rest"):
        for held in (fetched, swapped):
            answers.append(answer(held))
            start += answers[-1].shape[0]
    with jax.named_scope("combine"):
        cut = start - answers[-1].shape[0]
        early = jnp.concatenate(answers[:-1], axis=0)
        out = jnp.dot(dispatch[:, :cut], early, preferred_element_type=F32)
        out = out + jnp.dot(dispatch[:, cut:], answers[-1], preferred_element_type=F32)
    return out.astype(BF)[None]


def solution(mesh):
    placed = (
        P("doc", "seq", "tensor"),
        P("doc", "seq", "tensor", None),
        P(("doc", "seq"), "tensor"),
        P(("doc", "seq"), "tensor"),
        P(),
        P("doc", "seq", None),
        P("doc", None),
        P("doc", "seq"),
    )
    return jax.shard_map(
        shards, mesh=mesh, in_specs=placed, out_specs=P("doc", "seq", "tensor"), check_vma=False
    )
```

```python
import jax
import jax.numpy as jnp
from jax import lax
from jax.experimental import pallas as pl
from jax.experimental.pallas import tpu as pltpu
from jax.sharding import PartitionSpec as P

HD = 128
CAP = 8
BF = jnp.bfloat16
F32 = jnp.float32
HF = jnp.float16
NOTES = 8
KEY_SCALE = 2048.0
TOP_LEVEL = 14.0


def head_norm(x):
    return x * lax.rsqrt(jnp.mean(x * x, axis=-1, keepdims=True) + 1e-06)


def spread(v_ref, out_ref):
    n_doc, copies, _, width = out_ref.shape
    for d in range(n_doc):
        part = v_ref[:, d * width : (d + 1) * width]
        for t in range(copies):
            out_ref[d, t] = part


def spreading(v, n_doc, copies):
    vmem = pl.BlockSpec(memory_space=pltpu.VMEM)
    shape = (n_doc, copies, v.shape[0], v.shape[1] // n_doc)
    return pl.pallas_call(
        spread,
        out_shape=jax.ShapeDtypeStruct(shape, v.dtype),
        in_specs=[vmem],
        out_specs=vmem,
        compiler_params=pltpu.CompilerParams(vmem_limit_bytes=32 * 1024 * 1024),
    )(v)


def project(place_ref, x_ref, own_ref, other_ref, out_ref, w_ref):
    rows = w_ref.shape[0] // (own_ref.shape[0] * 2)
    half = own_ref.shape[0] // 2
    core, odd = place_ref[0], place_ref[1]
    for k, ref in enumerate((own_ref, other_ref)):
        for o in range(2):
            for j in range(half):
                owner = 2 * (2 * j + (o + odd) % 2) + (k + core) % 2
                at = pl.ds(pl.multiple_of(owner * rows, rows), rows)
                w_ref[at] = ref[o * half + j]
    out_ref[...] = jnp.dot(x_ref[...], w_ref[...], preferred_element_type=F32)


def projection(place, x, own, other):
    cols = own.shape[2]
    vmem = pl.BlockSpec(memory_space=pltpu.VMEM)
    return pl.pallas_call(
        project,
        out_shape=jax.ShapeDtypeStruct((x.shape[0], cols), F32),
        in_specs=[pl.BlockSpec(memory_space=pltpu.SMEM), vmem, vmem, vmem],
        out_specs=vmem,
        scratch_shapes=[pltpu.VMEM((x.shape[1], cols), BF)],
        compiler_params=pltpu.CompilerParams(vmem_limit_bytes=32 * 1024 * 1024),
    )(place, x, own, other)


def finish(len_ref, part_ref, out_ref):
    kv = part_ref[0]
    for d in range(1, part_ref.shape[0]):
        kv = kv + part_ref[d]
    vtok = kv.shape[0]
    keys = head_norm(kv[:, :HD]).astype(BF).astype(F32)
    values = kv[:, HD:].astype(BF).astype(F32)
    largest = jnp.max(jnp.max(jnp.abs(values), axis=1, keepdims=True), axis=0, keepdims=True)
    level = jnp.ceil(jnp.log2(jnp.maximum(largest, 1e-30)))
    length = jnp.full((NOTES, HD), len_ref[0, 0], jnp.int32).astype(F32)
    out_ref[:vtok, :HD] = keys * KEY_SCALE
    out_ref[:vtok, HD:] = values * jnp.exp2(TOP_LEVEL - level)
    out_ref[vtok:, :HD] = length
    out_ref[vtok:, HD:] = jnp.broadcast_to(level, (NOTES, HD))


def finishing(length, part):
    vmem = pl.BlockSpec(memory_space=pltpu.VMEM)
    return pl.pallas_call(
        finish,
        out_shape=jax.ShapeDtypeStruct((part.shape[1] + NOTES, part.shape[2]), F32),
        in_specs=[pl.BlockSpec(memory_space=pltpu.SMEM), vmem],
        out_specs=vmem,
        compiler_params=pltpu.CompilerParams(vmem_limit_bytes=32 * 1024 * 1024),
    )(length, part)


UNROLL = 8


def attend(gate_ref, q_ref, kv_ref, out_ref):
    heads = q_ref.shape[1] // HD
    vtok = kv_ref.shape[1] - 2 * NOTES
    pairs = kv_ref.shape[0] // 2
    factor = jnp.tanh(jnp.full((1, 1), gate_ref[0], F32))
    key = lax.broadcasted_iota(jnp.int32, (1, vtok), 1).astype(F32)
    four = (heads, 2, CAP, HD)

    def one(i):
        rows = pl.ds(pl.multiple_of(i * 2 * CAP, 2 * CAP), 2 * CAP)
        q = jnp.concatenate([q_ref[rows, h * HD : (h + 1) * HD] for h in range(heads)], axis=0)
        kv = kv_ref[pl.ds(2 * i, 2), :vtok].reshape(2 * vtok, 2 * HD)
        k, v = kv[:, :HD], kv[:, HD:]
        note = [kv_ref[2 * i + e, vtok:].astype(F32)[:1] for e in range(2)]
        s = lax.dot_general(q, k, (((1,), (1,)), ((), ())), preferred_element_type=F32)
        s = s.reshape(heads, 2, CAP, 2 * vtok) * (HD ** -0.5 / KEY_SCALE)
        s = [
            jnp.where((key < note[e][:, :HD])[None], s[:, e, :, e * vtok : (e + 1) * vtok], -jnp.inf)
            for e in range(2)
        ]
        s = jnp.stack(s, axis=1)
        top = jnp.max(s, axis=-1, keepdims=True)
        p = jnp.exp(s - top)
        total = jnp.sum(p, axis=-1, keepdims=True)
        zero = jnp.zeros_like(p[:, 0])
        left = jnp.stack([p[:, 0], zero], axis=1).reshape(-1, vtok)
        right = jnp.stack([zero, p[:, 1]], axis=1).reshape(-1, vtok)
        p = jnp.concatenate([left, right], axis=1).astype(BF)
        mixed = jnp.dot(p, v, preferred_element_type=F32)
        level = jnp.exp2(jnp.stack([n[:, HD:] for n in note])[None] - TOP_LEVEL)
        ans = mixed.reshape(four) * (factor / total) * level
        ans = ans.reshape(-1, HD).astype(BF)
        for h in range(heads):
            out_ref[rows, h * HD : (h + 1) * HD] = ans[h * 2 * CAP : (h + 1) * 2 * CAP]

    def body(i, carry):
        for u in range(unroll):
            one(i * unroll + u)
        return carry

    unroll = min(UNROLL, pairs)
    lax.fori_loop(0, pairs // unroll, body, 0)


def attention(gate, q, kv):
    smem = pl.BlockSpec(memory_space=pltpu.SMEM)
    vmem = pl.BlockSpec(memory_space=pltpu.VMEM)
    scores = q.size // HD * 2 * kv.shape[1]
    return pl.pallas_call(
        attend,
        out_shape=jax.ShapeDtypeStruct(q.shape, BF),
        in_specs=[smem, vmem, vmem],
        out_specs=vmem,
        cost_estimate=pl.CostEstimate(
            flops=4 * scores * HD, bytes_accessed=2 * kv.size, transcendentals=scores
        ),
        compiler_params=pltpu.CompilerParams(vmem_limit_bytes=32 * 1024 * 1024),
    )(gate, q, kv)


def shards(queries, vision, w_key, w_value, attn_gate, token_image, image_owner, image_len):
    n_doc = lax.axis_size("doc")
    n_seq = lax.axis_size("seq")
    n_z = n_seq // 2
    seq = lax.axis_index("seq")
    core = seq % 2
    z = seq // 2
    rows32, width = vision.shape[2], vision.shape[3]
    slice_w = width // n_doc
    swap = [(i, i ^ 1) for i in range(n_seq)]

    n_tensor = lax.axis_size("tensor")
    w = jnp.concatenate([w_key, w_value], axis=1)
    with jax.named_scope("vision_doc_tensor"):
        x = spreading(vision[0, 0], n_doc, n_tensor).reshape(-1, rows32, slice_w)
        x = lax.all_to_all(x, ("doc", "tensor"), split_axis=0, concat_axis=0, tiled=True)
        x = x.reshape(-1, slice_w)

    groups = [[2 * (2 * j + o) + c for j in range(n_z // 2)] for o in range(2) for c in range(2)]
    with jax.named_scope("weights_z"):
        near = lax.all_gather(w, "seq", axis=0, tiled=False, axis_index_groups=groups)
    near, token_image, x = lax.optimization_barrier((near, token_image, x))
    owners = jnp.arange(n_seq, dtype=jnp.int32)
    image_ids = token_image[0, :, 0]
    picked = image_ids[:, None] == owners[None, :]
    target = jnp.sum(jnp.where(picked, image_owner[0][None, :], 0), axis=1)
    onehot = (target[:, None] == owners[None, :]).astype(jnp.int32)
    ranks = jnp.cumsum(onehot, axis=0) - onehot
    slot = target * CAP + jnp.sum(ranks * onehot, axis=1)
    dispatch = (slot[:, None] == jnp.arange(n_seq * CAP, dtype=jnp.int32)[None, :]).astype(BF)
    with jax.named_scope("dispatch"):
        q = jnp.dot(dispatch.T, queries[0], preferred_element_type=F32).astype(BF)

    with jax.named_scope("weights_pair"):
        beside = lax.ppermute(near, "seq", [(i, i ^ 2) for i in range(n_seq)])
    own = jnp.concatenate([near, beside], axis=0)
    with jax.named_scope("weights_core"):
        other = lax.ppermute(own, "seq", swap)
    own, other, q = lax.optimization_barrier((own, other, q))
    with jax.named_scope("project"):
        part = projection(jnp.stack([core, z % 2]), x, own, other)
    with jax.named_scope("reduce_doc"):
        part = part.reshape(n_doc, -1, w.shape[1])
        part = lax.all_to_all(part, "doc", split_axis=0, concat_axis=0, tiled=True)

    with jax.named_scope("kv_seq"):
        block = finishing(image_len, part).astype(HF)
        blocks = lax.all_gather(block, "seq", axis=0, tiled=False).astype(BF)
    with jax.named_scope("attention"):
        answer = attention(attn_gate, q, jnp.pad(blocks, ((0, 0), (0, NOTES), (0, 0))))
    with jax.named_scope("combine"):
        out = jnp.dot(dispatch, answer, preferred_element_type=F32)
    return out.astype(BF)[None]


def solution(mesh):
    placed = (
        P("doc", "seq", "tensor"),
        P("doc", "seq", "tensor", None),
        P(("doc", "seq"), "tensor"),
        P(("doc", "seq"), "tensor"),
        P(),
        P("doc", "seq", None),
        P("doc", None),
        P("doc", "seq"),
    )
    return jax.shard_map(
        shards, mesh=mesh, in_specs=placed, out_specs=P("doc", "seq", "tensor"), check_vma=False
    )
```
